32 devices in a mesh: rep: 2 (over y), tp: 4 (over z), sp: 4 (over x, core).
Axes of the slice: x: 2, y: 2, z: 4, core: 2. Of those that a mesh axis runs over, the one named last changes fastest.
Arguments:
- hidden: bfloat16 [4096, 8192], P(('rep', 'sp'), 'tp'), parts along dimension 0, may hold values from -6 to 6
- doc_ids: int32 [4096], P(('rep', 'sp')), parts along dimension 0, may hold values from 0 to 3, never falling along the last dimension, each value on 1 to 1536 neighbouring positions
- gain: bfloat16 [8192], replicated, may hold values from 0.099609375 to 1.8984375
- w_query: bfloat16 [8192, 4096], P(None, 'tp'), may hold values from -3 to 3
- w_key: bfloat16 [8192, 512], P('tp'), as said below
- w_value: bfloat16 [8192, 512], P('tp'), may hold values from -0.0625 to 0.0625
- w_out: bfloat16 [4096, 8192], P('tp'), may hold values from -0.75 to 0.75
Outputs:
- layer_out: bfloat16 [4096, 8192], P(('rep', 'sp'), 'tp'), parts along dimension 0
The draws below stay inside these ranges and needn't reach their ends.
There are 2 independent parts, one for each index of `rep`. The reference program is written for one: setup_inputs(seed, part) draws one part's arguments, and reference() takes and returns one part's arrays. A program takes and returns all parts, laid end to end along the dimension named above; an argument that names none is the same for every part. Nothing has to cross between parts.
Inputs may be any that keep to these rules, and one draw needn't show every extreme that they name: `doc_ids`: ids never fall along the span; each prompt covers 1 to 1536 consecutive tokens, one exactly 1536. `w_key`: every entry lies within 6 / sqrt(8192) of zero.
All inputs are finite; a program needn't handle non-finite values.
Results may differ from the reference program's by a relative error of at most 0.019.
Values may be sent and summed in bfloat16 or wider, within the bound.
No kernel may reach another device: no remote copies, remote signals or barrier semaphores. Data moves between devices by JAX's collectives and lax.ppermute only.
A program may use at most 192 MiB of HBM per device.

```python
import math
import jax
import jax.numpy as jnp
import numpy as np
from jax import lax

D = 8192
HD = 128
HQ = 32
KV = 4
DOCS = 4
SEQ = 2048
MOST = 1536
N_TP = 4


def shared_keys(key):
    base = jax.random.normal(key, (D, KV * HD), jnp.float32)
    return jnp.clip(base, -6.0, 6.0) * D ** (-0.5)


def draw_w_key(key, part):
    return shared_keys(key).astype(jnp.bfloat16)


def draw_w_query(key, part):
    key = jax.random.fold_in(key, 7)
    noise_key = jax.random.fold_in(key, 0)
    noise = jnp.clip(jax.random.normal(noise_key, (D, HQ * HD), jnp.float32), -6.0, 6.0) * D ** (-0.5)
    return noise.astype(jnp.bfloat16)


def spiked(result, own_key, source, target, shards_of, factor):
    owner, partner = [(jnp.arange(result.shape[dim]) // (result.shape[dim] // shards_of)).reshape([-1 if axis == dim else 1 for axis in range(result.ndim)]) for dim in (source, target)]
    chosen = jax.random.permutation(own_key, shards_of)[partner]
    strong = (owner == chosen) | (owner == (partner + shards_of // 2) % shards_of)
    return jnp.where(strong, factor * result, result)


def block_levels(stream_key, dims, cuts, smallest, largest):
    loudness = 1.0
    for dim, shards_of in cuts:
        steps = jax.random.uniform(jax.random.fold_in(jax.random.fold_in(stream_key, 6), dim), (shards_of,), jnp.float32, smallest / len(cuts), largest / len(cuts))
        loudness = loudness * jnp.repeat(jnp.exp(steps), dims[dim] // shards_of).reshape((-1,) + (1,) * (len(dims) - 1 - dim))
    return loudness


def profile(count, total, most, skew):
    loads = [(1 << 20) // math.isqrt(rank ** skew) + 1 for rank in range(2, count + 1)]
    rest, counts = total - most - (count - 1), [1] * (count - 1)
    while rest > 0:
        candidates = [i for i in range(count - 1) if counts[i] < most]
        pool, budget = sum([loads[i] for i in candidates]), rest
        for i in candidates:
            more = min(most - counts[i], max(1, budget * loads[i] // pool), rest)
            counts[i] = counts[i] + more
            rest = rest - more
    return np.array([most] + counts)


def uneven(stream_key, number_of, total, most, slope):
    if number_of == 2:
        one = jax.random.randint(stream_key, (), max(1, total - most), min(most, total - 1) + 1)
        return jnp.stack([one, total - one])
    tallies = jnp.asarray(profile(number_of, total, most, slope), jnp.int32)
    pairs = (number_of - 1) // 2
    giver, sink = tallies[1:1 + 2 * pairs:2], tallies[2:2 + 2 * pairs:2]
    margin = jnp.minimum(giver - 1, most - sink)
    moved = jax.random.randint(jax.random.fold_in(stream_key, 1), (pairs,), 0, 1 << 20) % (margin + 1)
    tallies = tallies.at[1:1 + 2 * pairs:2].set(giver - moved).at[2:2 + 2 * pairs:2].set(sink + moved)
    return tallies[jax.random.permutation(jax.random.fold_in(stream_key, 2), number_of)]


def scatter_about(stream_key, dims, deviation, limit, cuts=(), held_as=jnp.bfloat16):
    factor_of = block_levels(stream_key, dims, cuts, -0.22, 0.18) if cuts else 1.0
    drawn = jax.random.normal(stream_key, dims, jnp.float32) * deviation * factor_of
    return jnp.minimum(jnp.maximum(drawn, -limit), limit).astype(held_as)


def bell_draw_with(stream_key, dims, spread, reach, cuts, heavy, kind=jnp.bfloat16):
    entries = spread * jax.random.normal(stream_key, dims, jnp.float32)
    if cuts:
        entries = entries * block_levels(stream_key, dims, cuts, -0.22, 0.18)
    return jnp.clip(spiked(entries, jax.random.fold_in(stream_key, 3), *heavy), -reach, reach).astype(kind)


def setup_inputs(seed: int = 0, part: int = 0) -> dict:
    key_of = jax.random.split(jax.random.key(seed), 8)
    part_splits = jax.random.split(jax.random.fold_in(key_of[7], part), 8)
    return {
        "hidden": scatter_about(part_splits[0], (SEQ, D), 1.0, 6.0, ((0, 4), (1, 4))),
        "doc_ids": jnp.searchsorted(jnp.cumsum(uneven(part_splits[1], DOCS, SEQ, MOST, 2)), jnp.arange(SEQ), side="right").astype(jnp.int32),
        "gain": jnp.clip(1.0 + 0.18 * jax.random.normal(key_of[2], (D,), jnp.float32), 0.099609375, 1.8984375).astype(jnp.bfloat16),
        "w_query": draw_w_query(jax.random.fold_in(key_of[7], 71), part),
        "w_key": draw_w_key(jax.random.fold_in(key_of[7], 71), part),
        "w_value": scatter_about(key_of[5], (D, KV * HD), D ** -0.5, 0.0625, ((0, 4),)),
        "w_out": bell_draw_with(key_of[6], (HQ * HD, D), HD ** -0.5, 0.75, ((0, 4),), (0, 1, 4, 2.0)),
    }


rope_base = 500000.0
norm_eps = 1e-05
masked_score = -1e+30

def rotate(field, positions):
    half_dim = field.shape[-1] // 2
    steps_index = jnp.arange(half_dim, dtype=jnp.float32)
    frequency = jnp.power(rope_base, -2.0 * steps_index / field.shape[-1])
    angles = positions.astype(jnp.float32)[:, None] * frequency[None, :]
    cosine = jnp.cos(angles)[:, None, :]
    sine = jnp.sin(angles)[:, None, :]
    first_half = field[..., :half_dim]
    second_half = field[..., half_dim:]
    return jnp.concatenate([first_half * cosine - second_half * sine, second_half * cosine + first_half * sine], axis=-1)

def doc_starts(all_ids):
    labels = jnp.arange(DOCS, dtype=jnp.int32)
    return lax.optimization_barrier(jnp.sum((all_ids[None, :] < labels[:, None]).astype(jnp.int32), axis=1))

def positions_of(token_ids, token_index, starts):
    labels = jnp.arange(DOCS, dtype=jnp.int32)
    member = token_ids[:, None] == labels[None, :]
    first_index = lax.optimization_barrier(jnp.sum(jnp.where(member, starts[None, :], 0), axis=1))
    return (token_index - first_index).astype(jnp.int32)

def settle(value):
    return lax.optimization_barrier(value.astype(jnp.bfloat16)).astype(jnp.float32)

def reference(hidden, doc_ids, gain, w_query, w_key, w_value, w_out):
    seq_rows = hidden.shape[0]
    hidden_f = hidden.astype(jnp.float32)
    inverse = lax.rsqrt(lax.optimization_barrier(jnp.mean(hidden_f * hidden_f, axis=1, keepdims=True)) + norm_eps)
    normed = (hidden_f * inverse * gain.astype(jnp.float32)[None, :]).astype(jnp.bfloat16)
    query_flat = jnp.dot(normed, w_query, preferred_element_type=jnp.float32)
    slice_width = D // N_TP
    key_sum = jnp.zeros((seq_rows, KV * HD), jnp.float32)
    value_sum = jnp.zeros((seq_rows, KV * HD), jnp.float32)
    for block in range(N_TP):
        columns = normed[:, block * slice_width:(block + 1) * slice_width]
        key_rows = w_key[block * slice_width:(block + 1) * slice_width]
        value_rows = w_value[block * slice_width:(block + 1) * slice_width]
        key_sum = key_sum + settle(jnp.dot(columns, key_rows, preferred_element_type=jnp.float32))
        value_sum = value_sum + settle(jnp.dot(columns, value_rows, preferred_element_type=jnp.float32))
    token_index = jnp.arange(seq_rows, dtype=jnp.int32)
    positions = positions_of(doc_ids, token_index, doc_starts(doc_ids))
    queries = rotate(query_flat.reshape(seq_rows, HQ, HD), positions).astype(jnp.bfloat16)
    keys = rotate(key_sum.reshape(seq_rows, KV, HD), positions).astype(jnp.bfloat16)
    values = value_sum.reshape(seq_rows, KV, HD).astype(jnp.bfloat16)
    visible = (doc_ids[:, None] == doc_ids[None, :]) & (token_index[:, None] >= token_index[None, :])
    group_size = HQ // KV
    scale = HD ** (-0.5)

    def one_head(head):
        query_head = lax.dynamic_index_in_dim(queries, head, 1, False)
        key_head = lax.dynamic_index_in_dim(keys, head // group_size, 1, False)
        value_head = lax.dynamic_index_in_dim(values, head // group_size, 1, False)
        scores = jnp.dot(query_head, key_head.T, preferred_element_type=jnp.float32) * scale
        scores = jnp.where(visible, scores, masked_score)
        row_max = lax.optimization_barrier(jnp.max(scores, axis=1, keepdims=True))
        exps = jnp.where(visible, jnp.exp(scores - row_max), 0.0)
        total = lax.optimization_barrier(jnp.sum(exps, axis=1, keepdims=True))
        mixed = jnp.dot(exps.astype(jnp.bfloat16), value_head, preferred_element_type=jnp.float32)
        return (mixed / total).astype(jnp.bfloat16)
    attended = lax.map(one_head, jnp.arange(HQ, dtype=jnp.int32))
    flat = jnp.transpose(attended, (1, 0, 2)).reshape(seq_rows, HQ * HD)
    head_width = HQ * HD // N_TP
    projected = jnp.zeros((seq_rows, D), jnp.float32)
    for block in range(N_TP):
        columns = flat[:, block * head_width:(block + 1) * head_width]
        weight_rows = w_out[block * head_width:(block + 1) * head_width]
        projected = projected + settle(jnp.dot(columns, weight_rows, preferred_element_type=jnp.float32))
    return (hidden_f + projected).astype(jnp.bfloat16)
```

```python
import jax
import jax.numpy as jnp
from jax import lax
from jax.sharding import PartitionSpec as P

HD = 128
HQ = 32
KV = 4
DOCS = 4
CHUNKS = 4

rope_base = 500000.0
norm_eps = 1e-05
masked_score = -1e30


def angles_of(positions):
    half_dim = HD // 2
    steps_index = jnp.arange(half_dim, dtype=jnp.float32)
    frequency = jnp.power(rope_base, -2.0 * steps_index / HD)
    angles = positions.astype(jnp.float32)[:, None] * frequency[None, :]
    return jnp.cos(angles), jnp.sin(angles)


def rotate(field, cosine, sine):
    half_dim = HD // 2
    first_half = field[..., :half_dim]
    second_half = field[..., half_dim:]
    return jnp.concatenate(
        [first_half * cosine - second_half * sine, second_half * cosine + first_half * sine],
        axis=-1,
    )


def line_gather(own, count, rank):
    from_low, from_high = [], []
    up, down = own, own
    for step in range(1, count):
        up = lax.ppermute(up, "tp", [(i, i + 1) for i in range(step - 1, count - 1)])
        down = lax.ppermute(down, "tp", [(i, i - 1) for i in range(1, count - step + 1)])
        from_low.append(up)
        from_high.append(down)
    blocks = []
    for block in range(count):
        value = own
        for step in range(1, count):
            if block + step < count:
                value = jnp.where(rank == block + step, from_low[step - 1], value)
            if block - step >= 0:
                value = jnp.where(rank == block - step, from_high[step - 1], value)
        blocks.append(value)
    return jnp.concatenate(blocks, axis=1)


def line_scatter(take, count, rank):
    up = down = None
    for step in range(1, count):
        mine_up = take(jnp.minimum(rank + count - step, count - 1))
        mine_down = take(jnp.maximum(rank - count + step, 0))
        if up is not None:
            mine_up = (mine_up.astype(jnp.float32) + up.astype(jnp.float32)).astype(jnp.bfloat16)
            mine_down = (mine_down.astype(jnp.float32) + down.astype(jnp.float32)).astype(jnp.bfloat16)
        up = lax.ppermute(mine_up, "tp", [(i, i + 1) for i in range(step)])
        down = lax.ppermute(mine_down, "tp", [(i, i - 1) for i in range(count - step, count)])
    own = take(rank).astype(jnp.float32)
    return own + up.astype(jnp.float32) + down.astype(jnp.float32)


def make_body(count, sp_count):
    def body(hidden, doc_ids, gain, w_query, w_key, w_value, w_out):
        rows, width = hidden.shape
        rank = lax.axis_index("tp")
        sp_rank = lax.axis_index("sp")
        heads = w_query.shape[1] // HD
        group = HQ // KV
        model = width * count
        scale = HD ** (-0.5)
        gain_own = lax.dynamic_slice_in_dim(gain, rank * width, width, 0).astype(jnp.float32)
        hidden_f = hidden.astype(jnp.float32)
        scaled = (hidden_f * gain_own[None, :]).astype(jnp.bfloat16)
        squares = lax.psum(jnp.sum(hidden_f * hidden_f, axis=1), "tp")
        inverse = lax.rsqrt(squares / model + norm_eps)[:, None]

        all_ids = lax.all_gather(doc_ids, "sp", axis=0, tiled=True)
        labels = jnp.arange(DOCS, dtype=jnp.int32)
        starts = jnp.sum((all_ids[None, :] < labels[:, None]).astype(jnp.int32), axis=1)
        own_index = sp_rank * rows + jnp.arange(rows, dtype=jnp.int32)
        first = jnp.sum(jnp.where(doc_ids[:, None] == labels[None, :], starts[None, :], 0), axis=1)
        cosine, sine = angles_of(own_index - first)

        key_part = jnp.dot(scaled, w_key, preferred_element_type=jnp.float32).astype(jnp.bfloat16)
        value_part = jnp.dot(scaled, w_value, preferred_element_type=jnp.float32).astype(jnp.bfloat16)

        def take_kv(d):
            head = d * heads // group
            return jnp.concatenate(
                [
                    lax.dynamic_slice_in_dim(key_part, head * HD, HD, 1),
                    lax.dynamic_slice_in_dim(value_part, head * HD, HD, 1),
                ],
                axis=1,
            )

        kv = line_scatter(take_kv, count, rank) * inverse
        keys = rotate(kv[:, :HD], cosine, sine).astype(jnp.bfloat16)
        values = kv[:, HD:].astype(jnp.bfloat16)
        both = lax.all_gather(jnp.concatenate([keys, values], axis=1), "sp", axis=0, tiled=True)
        keys, values = both[:, :HD], both[:, HD:]
        key_index = jnp.arange(both.shape[0], dtype=jnp.int32)

        chunk = rows // CHUNKS
        outs = []
        for c in range(CHUNKS):
            part = slice(c * chunk, (c + 1) * chunk)
            whole = line_gather(scaled[part], count, rank)
            query = jnp.dot(whole, w_query, preferred_element_type=jnp.float32) * inverse[part]
            query = rotate(
                query.reshape(chunk, heads, HD), cosine[part][:, None, :], sine[part][:, None, :]
            ).astype(jnp.bfloat16)
            scores = (
                jnp.einsum("qhd,kd->qhk", query, keys, preferred_element_type=jnp.float32) * scale
            )
            visible = (key_index[None, :] <= own_index[part][:, None]) & (
                key_index[None, :] >= first[part][:, None]
            )
            scores = jnp.where(visible[:, None, :], scores, masked_score)
            exps = jnp.exp(scores - jnp.max(scores, axis=2, keepdims=True))
            exps = jnp.where(visible[:, None, :], exps, 0.0)
            total = jnp.sum(exps, axis=2)
            mixed = jnp.einsum(
                "qhk,kd->qhd", exps.astype(jnp.bfloat16), values, preferred_element_type=jnp.float32
            )
            flat = (mixed / total[..., None]).astype(jnp.bfloat16).reshape(chunk, heads * HD)
            partial = jnp.dot(flat, w_out, preferred_element_type=jnp.float32).astype(jnp.bfloat16)

            def take(d, partial=partial):
                return lax.dynamic_slice_in_dim(partial, d * width, width, 1)

            summed = line_scatter(take, count, rank)
            outs.append((hidden_f[part] + summed).astype(jnp.bfloat16))
        return jnp.concatenate(outs, axis=0)

    return body


def solution(mesh):
    placed = (
        P(("rep", "sp"), "tp"),
        P(("rep", "sp")),
        P(),
        P(None, "tp"),
        P("tp", None),
        P("tp", None),
        P("tp", None),
    )
    body = make_body(mesh.shape["tp"], mesh.shape["sp"])
    return jax.shard_map(
        body, mesh=mesh, in_specs=placed, out_specs=P(("rep", "sp"), "tp"), check_vma=False
    )
```

```python
import functools

import jax
import jax.numpy as jnp
from jax import lax
from jax.experimental import pallas as pl
from jax.experimental.pallas import tpu as pltpu
from jax.sharding import PartitionSpec as P

HD = 128
HQ = 32
KV = 4
DOCS = 4
PERIODS = 2
STREAMS = 2

rope_base = 500000.0
norm_eps = 1e-05
masked_score = -1e30
log2_e = 1.4426950408889634
VMEM_LIMIT = 46 * 1024 * 1024
BLOCK = 512
VMEM = pl.BlockSpec(memory_space=pltpu.VMEM)
SMEM = pl.BlockSpec(memory_space=pltpu.SMEM)
ANY = pl.BlockSpec(memory_space=pl.ANY)


def rope_tables(positions):
    half_dim = HD // 2
    steps_index = jnp.arange(half_dim, dtype=jnp.float32)
    frequency = jnp.power(rope_base, -2.0 * steps_index / HD)
    angles = positions.astype(jnp.float32)[:, None] * frequency[None, :]
    cosine, sine = jnp.cos(angles), jnp.sin(angles)
    return jnp.concatenate([cosine, cosine], axis=1), jnp.concatenate([-sine, sine], axis=1)


def rotate(field, cosine, sine):
    half_dim = HD // 2
    swapped = jnp.concatenate([field[..., half_dim:], field[..., :half_dim]], axis=-1)
    return field * cosine + swapped * sine


def chunk_kernel(count, pieces_of, low, info_ref, *refs):
    total_pieces = len(pieces_of) + 1
    pieces = refs[:total_pieces]
    w_query, w_out, table, both, out = refs[total_pieces : total_pieces + 5]
    held, query_w, out_w, rows_table, kv, query, top, acc, flat, sems, q_sems, o_sems = refs[
        total_pieces + 5 :
    ]
    rows = held.shape[0]
    width = held.shape[1] // count
    parts, depth, piece_columns = query_w.shape[0], query_w.shape[1], query_w.shape[2]
    heads = query.shape[0]
    rank, start, base = info_ref[0], info_ref[1], info_ref[2]
    even = rank % 2 == 0

    def place(source, block):
        columns = pl.ds(pl.multiple_of(block * width, width), width)
        return pltpu.make_async_copy(source, held.at[:, columns], sems.at[block])

    place(pieces[0].at[pl.ds(low, rows)], rank).start()
    for piece, (kind, step) in zip(pieces[1:], pieces_of):
        block = jnp.where(even == (kind == "outer"), rank + step, rank - step)

        @pl.when((block >= 0) & (block < count))
        def _():
            place(piece, block).start()

    def query_copy(k):
        return pltpu.make_async_copy(
            w_query.at[:, pl.ds(pl.multiple_of(k * piece_columns, piece_columns), piece_columns)],
            query_w.at[k],
            q_sems.at[k],
        )

    for k in range(parts):
        query_copy(k).start()
    table_copy = pltpu.make_async_copy(table.at[pl.ds(low, rows)], rows_table, sems.at[count])
    table_copy.start()
    kv_copy = pltpu.make_async_copy(both, kv, sems.at[count + 1])
    kv_copy.start()
    out_parts = out_w.shape[0]
    out_columns = out_w.shape[2]

    def out_copy(k):
        return pltpu.make_async_copy(
            w_out.at[:, pl.ds(pl.multiple_of(k * out_columns, out_columns), out_columns)],
            out_w.at[k],
            o_sems.at[k],
        )

    for k in range(out_parts):
        out_copy(k).start()

    for block in range(count):
        place(pieces[0].at[pl.ds(low, rows)], block).wait()
    table_copy.wait()
    cos, sin = rows_table[:, :HD], rows_table[:, HD : 2 * HD]
    pair = piece_columns // HD

    @pl.loop(0, parts)
    def _(k):
        query_copy(k).wait()
        total = jnp.dot(held[...], query_w[k], preferred_element_type=jnp.float32)
        for h in range(pair):
            field = total[:, h * HD : (h + 1) * HD]
            swapped = pltpu.roll(field, HD // 2, 1)
            query[k * pair + h] = (field * cos + swapped * sin).astype(jnp.bfloat16)

    kv_copy.wait()
    factor = HD ** (-0.5) * log2_e
    top[...] = jnp.full_like(top, masked_score)
    acc[...] = jnp.zeros_like(acc)
    first = rows_table[:, 2 * HD : 2 * HD + 1].astype(jnp.int32)
    row_index = base + low + lax.broadcasted_iota(jnp.int32, (rows, BLOCK), 0)
    column = lax.broadcasted_iota(jnp.int32, (rows, BLOCK), 1)
    ones = jnp.ones((BLOCK, HD), jnp.bfloat16)

    def step(j, carry):
        offset = pl.multiple_of(j * BLOCK, BLOCK)
        key_index = column + offset
        bias = jnp.where((key_index <= row_index) & (key_index >= first), 0.0, masked_score)
        key = kv[pl.ds(offset, BLOCK), :HD]
        value = jnp.concatenate([kv[pl.ds(offset, BLOCK), HD:], ones], axis=1)
        for h in range(heads):
            scores = lax.dot_general(
                query[h], key, (((1,), (1,)), ((), ())), preferred_element_type=jnp.float32
            )
            scores = scores * factor + bias
            old = top[h]
            new = jnp.maximum(old, jnp.max(scores, axis=1, keepdims=True))
            exps = jnp.exp2(scores - new[:, :1])
            mixed = jnp.dot(exps.astype(jnp.bfloat16), value, preferred_element_type=jnp.float32)
            keep = jnp.exp2(old - new)
            acc[h] = acc[h] * jnp.concatenate([keep, keep], axis=1) + mixed
            top[h] = new
        return carry

    lax.fori_loop(start, (base + low + rows - 1) // BLOCK + 1, step, 0)
    for h in range(heads):
        flat[:, h * HD : (h + 1) * HD] = (acc[h, :, :HD] / acc[h, :, HD:]).astype(jnp.bfloat16)

    per_block = width // out_columns

    @pl.loop(0, count)
    def _(b):
        for k in range(per_block):
            out_copy(b * per_block + k).wait()
            out[b, :, k * out_columns : (k + 1) * out_columns] = jnp.dot(
                flat[...], out_w[b * per_block + k], preferred_element_type=jnp.float32
            ).astype(jnp.bfloat16)


def chunk_terms(count, low, rows, scaled, arrived, info, w_query, w_out, table, both):
    width = scaled.shape[1]
    model, columns = w_query.shape
    inner = w_out.shape[0]
    heads = columns // HD
    tokens = both.shape[0]
    pieces = [scaled] + [piece for _, _, piece in arrived]
    pieces_of = [(kind, step) for kind, step, _ in arrived]
    q_columns = min(columns, 256)
    o_columns = min(width, 1024)
    q_parts, o_parts = columns // q_columns, model // o_columns
    return pl.pallas_call(
        functools.partial(chunk_kernel, count, pieces_of, low),
        out_shape=jax.ShapeDtypeStruct((count, rows, width), jnp.bfloat16),
        in_specs=[SMEM] + [ANY] * (len(pieces) + 4),
        out_specs=VMEM,
        scratch_shapes=[
            pltpu.VMEM((rows, model), jnp.bfloat16),
            pltpu.VMEM((q_parts, model, q_columns), jnp.bfloat16),
            pltpu.VMEM((o_parts, inner, o_columns), jnp.bfloat16),
            pltpu.VMEM((rows, 3 * HD), jnp.float32),
            pltpu.VMEM((tokens, 2 * HD), jnp.bfloat16),
            pltpu.VMEM((heads, rows, HD), jnp.bfloat16),
            pltpu.VMEM((heads, rows, HD), jnp.float32),
            pltpu.VMEM((heads, rows, 2 * HD), jnp.float32),
            pltpu.VMEM((rows, inner), jnp.bfloat16),
            pltpu.SemaphoreType.DMA((count + 2,)),
            pltpu.SemaphoreType.DMA((q_parts,)),
            pltpu.SemaphoreType.DMA((o_parts,)),
        ],
        compiler_params=pltpu.CompilerParams(vmem_limit_bytes=VMEM_LIMIT),
        cost_estimate=pl.CostEstimate(
            flops=4 * rows * model * columns, bytes_accessed=4 * model * columns, transcendentals=0
        ),
        name="chunk_terms",
    )(info, *pieces, w_query, w_out, table, both)


def finish_kernel(count, low, has_inner, info_ref, hidden, terms, outer, inner, *refs):
    out, a, b, c, d, total, sems = refs[-7:]
    rows = a.shape[0]
    rank = info_ref[0]
    copies = [
        pltpu.make_async_copy(source, target, sems.at[k])
        for k, (source, target) in enumerate(
            [(hidden.at[pl.ds(low, rows)], a), (terms.at[rank], b), (outer, c), (inner, d)]
        )
    ]
    for copy in copies:
        copy.start()
    for copy in copies:
        copy.wait()
    summed = b[...].astype(jnp.float32) + c[...].astype(jnp.float32)
    middle = (rank > 0) & (rank < count - 1)
    other = jnp.where(middle, d[...].astype(jnp.float32), 0.0)
    total[...] = (a[...].astype(jnp.float32) + (summed + other)).astype(jnp.bfloat16)
    copy = pltpu.make_async_copy(total, out.at[pl.ds(low, rows)], sems.at[4])
    copy.start()
    copy.wait()


def finish(count, low, info, hidden, terms, last, out):
    _, rows, width = terms.shape
    outer, inner = last
    operands = [info, hidden, terms, outer, inner if inner is not None else outer]
    aliases = {}
    if out is not None:
        aliases = {len(operands): 0}
        operands.append(out)
    return pl.pallas_call(
        functools.partial(finish_kernel, count, low, inner is not None),
        out_shape=jax.ShapeDtypeStruct(hidden.shape, jnp.bfloat16),
        in_specs=[SMEM] + [ANY] * (len(operands) - 1),
        out_specs=ANY,
        scratch_shapes=[pltpu.VMEM((rows, width), jnp.bfloat16)] * 5 + [pltpu.SemaphoreType.DMA((5,))],
        input_output_aliases=aliases,
        compiler_params=pltpu.CompilerParams(vmem_limit_bytes=VMEM_LIMIT),
        name="finish",
    )(*operands)


def after(value, *others):
    return lax.optimization_barrier((value, others))[0]


def all_sum(value, axis, size):
    distance = 1
    while distance < size:
        value = value + lax.ppermute(value, axis, [(i, i ^ distance) for i in range(size)])
        distance *= 2
    return value


class Line:
    def __init__(self, count, sp_count, rank):
        self.count, self.rank = count, rank
        self.even = rank % 2 == 0
        self.middle = (rank > 0) & (rank < count - 1)
        self.outer_pairs = [(i, i ^ 1) for i in range(count)]
        self.inner_pairs = []
        for i in range(count):
            for s in range(sp_count):
                partner = i + 1 if i % 2 else i - 1
                if 0 < i < count - 1:
                    self.inner_pairs.append((i * sp_count + s, partner * sp_count + s))
                else:
                    self.inner_pairs.append((i * sp_count + s, i * sp_count + (s ^ 1)))

    def outer(self, value):
        return lax.ppermute(value, "tp", self.outer_pairs)

    def inner(self, value):
        return lax.ppermute(value, ("tp", "sp"), self.inner_pairs)

    def term(self, terms, upward, step):
        dest = jnp.where(upward, self.rank + self.count - step, self.rank - self.count + step)
        valid = (dest >= 0) & (dest < self.count)
        return lax.dynamic_index_in_dim(terms, jnp.clip(dest, 0, self.count - 1), 0, False), valid

    def round(self, step, own, terms, last):
        count = self.count
        from_outer, from_inner = last
        gather_outer = own is not None and step < count
        gather_inner = own is not None and step < count - 1
        scatter_outer = terms is not None and step > 1
        scatter_inner = terms is not None and step > 2
        to_outer = to_inner = None
        if gather_outer:
            to_outer = own if step == 1 else from_inner
        if gather_inner:
            to_inner = own if step == 1 else from_outer
        if scatter_outer:
            mine, valid = self.term(terms, self.even, step - 1)
            if step > 3:
                added = (mine.astype(jnp.float32) + from_inner.astype(jnp.float32)).astype(jnp.bfloat16)
                mine = jnp.where(self.middle, added, mine)
            to_outer = mine if to_outer is None else jnp.where(valid, mine, to_outer)
        if scatter_inner:
            mine, valid = self.term(terms, ~self.even, step - 1)
            mine = (mine.astype(jnp.float32) + from_outer.astype(jnp.float32)).astype(jnp.bfloat16)
            to_inner = mine if to_inner is None else jnp.where(valid, mine, to_inner)
        got_outer = None if to_outer is None else self.outer(to_outer)
        got_inner = None if to_inner is None else self.inner(to_inner)
        return got_outer, got_inner

    def scatter_only(self, step, terms, last):
        count = self.count
        from_outer, from_inner = last
        mine, _ = self.term(terms, self.even, step)
        if step > 2:
            added = (mine.astype(jnp.float32) + from_inner.astype(jnp.float32)).astype(jnp.bfloat16)
            mine = jnp.where(self.middle, added, mine)
        if step < count - 1:
            pairs = [
                (i, i ^ 1) for i in range(count) if (i <= step - 1 if i % 2 == 0 else i >= count - step)
            ]
            got_outer = lax.ppermute(mine, "tp", pairs)
        else:
            got_outer = self.outer(mine)
        if step < 2:
            return got_outer, None
        mine, _ = self.term(terms, ~self.even, step)
        mine = (mine.astype(jnp.float32) + from_outer.astype(jnp.float32)).astype(jnp.bfloat16)
        return got_outer, self.inner(mine)

    def total(self, terms, last):
        mine = lax.dynamic_index_in_dim(terms, self.rank, 0, False).astype(jnp.float32)
        mine = mine + last[0].astype(jnp.float32)
        return jnp.where(self.middle, mine + last[1].astype(jnp.float32), mine)


def make_body(count, sp_count):
    def body(hidden, doc_ids, gain, w_query, w_key, w_value, w_out):
        rows, width = hidden.shape
        rank = lax.axis_index("tp")
        sp_rank = lax.axis_index("sp")
        heads = w_query.shape[1] // HD
        group = HQ // KV
        model = width * count
        line = Line(count, sp_count, rank)
        gain_own = lax.dynamic_slice_in_dim(gain, rank * width, width, 0).astype(jnp.float32)
        hidden_f = hidden.astype(jnp.float32)
        scaled = (hidden_f * gain_own[None, :]).astype(jnp.bfloat16)
        squares = all_sum(jnp.sum(hidden_f * hidden_f, axis=1), "tp", count)
        inverse = lax.rsqrt(squares / model + norm_eps)[:, None]
        w_query = pltpu.with_memory_space_constraint(w_query, pltpu.HBM)
        w_out = pltpu.with_memory_space_constraint(w_out, pltpu.HBM)
        chunk = rows // (PERIODS * STREAMS)

        labels = jnp.arange(DOCS, dtype=jnp.int32)
        starts = all_sum(
            jnp.sum((doc_ids[None, :] < labels[:, None]).astype(jnp.int32), axis=1), "sp", sp_count
        )
        base = sp_rank * rows
        own_index = base + jnp.arange(rows, dtype=jnp.int32)
        first = jnp.sum(jnp.where(doc_ids[:, None] == labels[None, :], starts[None, :], 0), axis=1)
        cosine, sine = rope_tables(own_index - first)
        table = jnp.concatenate(
            [
                cosine * inverse,
                sine * inverse,
                jnp.broadcast_to(first.astype(jnp.float32)[:, None], (rows, HD)),
            ],
            axis=1,
        )
        infos = [
            jnp.stack([rank, first[k * chunk] // BLOCK, base]).astype(jnp.int32)
            for k in range(PERIODS * STREAMS)
        ]

        key_part = jnp.dot(scaled, w_key, preferred_element_type=jnp.float32).astype(jnp.bfloat16)
        value_part = jnp.dot(scaled, w_value, preferred_element_type=jnp.float32).astype(jnp.bfloat16)
        kv_terms = []
        for d in range(count):
            head = slice(d * heads // group * HD, (d * heads // group + 1) * HD)
            kv_terms.append(jnp.concatenate([key_part[:, head], value_part[:, head]], axis=1))
        kv_terms = jnp.stack(kv_terms)
        kv_last = (None, None)

        out = None
        both = None
        last = [(None, None)] * STREAMS
        terms = [None] * STREAMS
        for period in range(PERIODS + 1):
            gather = period < PERIODS
            owns = [None] * STREAMS
            arrived = [[] for _ in range(STREAMS)]
            fresh = [None] * STREAMS
            for step in range(1, count + 1):
                if period == 0 and step < count:
                    kv_last = line.scatter_only(step, kv_terms, kv_last)
                for j in range(STREAMS):
                    if not (gather and step < count) and not (terms[j] is not None and step > 1):
                        continue
                    if gather and step == 1:
                        low = (period * STREAMS + j) * chunk
                        owns[j] = scaled[low : low + chunk]
                        if period:
                            owns[j] = after(owns[j], last[j], terms[:j])
                    last[j] = line.round(step, owns[j], terms[j], last[j])
                    if gather and step < count:
                        arrived[j].append(("outer", step, last[j][0]))
                        if step < count - 1:
                            arrived[j].append(("inner", step, last[j][1]))
            if period == 0:
                kv = line.total(kv_terms, kv_last) * inverse
                keys = rotate(kv[:, :HD], cosine, sine).astype(jnp.bfloat16)
                both = jnp.concatenate([keys, kv[:, HD:].astype(jnp.bfloat16)], axis=1)
                both = lax.all_gather(both, "sp", axis=0, tiled=True)
            for j in range(STREAMS):
                if terms[j] is not None:
                    low = ((period - 1) * STREAMS + j) * chunk
                    out = finish(count, low, infos[0], hidden, terms[j], last[j], out)
                if gather:
                    k = period * STREAMS + j
                    terms[j] = chunk_terms(
                        count, k * chunk, chunk, scaled, arrived[j], infos[k], w_query, w_out, table, both
                    )
        return out

    return body


def solution(mesh):
    placed = (
        P(("rep", "sp"), "tp"),
        P(("rep", "sp")),
        P(),
        P(None, "tp"),
        P("tp", None),
        P("tp", None),
        P("tp", None),
    )
    body = make_body(mesh.shape["tp"], mesh.shape["sp"])
    return jax.shard_map(
        body, mesh=mesh, in_specs=placed, out_specs=P(("rep", "sp"), "tp"), check_vma=False
    )
```

```python
import functools

import jax
import jax.numpy as jnp
from jax import lax
from jax.experimental import pallas as pl
from jax.experimental.pallas import tpu as pltpu
from jax.sharding import PartitionSpec as P

HD = 128
HQ = 32
KV = 4
DOCS = 4
PERIODS = 2
STREAMS = 2

rope_base = 500000.0
norm_eps = 1e-05
masked_score = -1e30
log2_e = 1.4426950408889634
VMEM_LIMIT = 46 * 1024 * 1024
GROUP = 2
BLOCK = 1024
VMEM = pl.BlockSpec(memory_space=pltpu.VMEM)
SMEM = pl.BlockSpec(memory_space=pltpu.SMEM)
ANY = pl.BlockSpec(memory_space=pl.ANY)


def rope_tables(positions):
    half_dim = HD // 2
    steps_index = jnp.arange(half_dim, dtype=jnp.float32)
    frequency = jnp.power(rope_base, -2.0 * steps_index / HD)
    angles = positions.astype(jnp.float32)[:, None] * frequency[None, :]
    cosine, sine = jnp.cos(angles), jnp.sin(angles)
    return jnp.concatenate([cosine, cosine], axis=1), jnp.concatenate([-sine, sine], axis=1)


def rotate(field, cosine, sine):
    half_dim = HD // 2
    swapped = jnp.concatenate([field[..., half_dim:], field[..., :half_dim]], axis=-1)
    return field * cosine + swapped * sine


def in_hbm(value):
    return pltpu.with_memory_space_constraint(value, pltpu.HBM)


def wait_for(target, sem):
    pltpu.make_async_copy(target, target, sem).wait()


def chunk_kernel(count, pieces_of, low, info_ref, *refs):
    total_pieces = len(pieces_of) + 1
    pieces = refs[:total_pieces]
    w_query, w_out, table = refs[total_pieces : total_pieces + 3]
    kv_pieces = refs[total_pieces + 3 : -13]
    out, held, query_w, out_w, rows_table, kv, query, top, acc, flat, sems, q_sems, o_sems = refs[-13:]
    rows = held.shape[0]
    width = held.shape[1] // count
    parts, depth, piece_columns = query_w.shape[0], query_w.shape[1], query_w.shape[2]
    heads = query.shape[0] // rows
    rank, start, sp_rank = info_ref[0], info_ref[1], info_ref[2]
    span = kv_pieces[0].shape[0]
    base = sp_rank * span
    even = rank % 2 == 0

    def place(source, block):
        columns = pl.ds(pl.multiple_of(block * width, width), width)
        return pltpu.make_async_copy(source, held.at[:, columns], sems.at[0])

    place(pieces[0].at[pl.ds(low, rows)], rank).start()
    for piece, (kind, step) in zip(pieces[1:], pieces_of):
        block = jnp.where(even == (kind == "outer"), rank + step, rank - step)

        @pl.when((block >= 0) & (block < count))
        def _():
            place(piece, block).start()

    def query_copy(k):
        return pltpu.make_async_copy(
            w_query.at[:, pl.ds(pl.multiple_of(k * piece_columns, piece_columns), piece_columns)],
            query_w.at[k],
            q_sems.at[k * q_sems.shape[0] // parts],
        )

    for k in range(parts):
        query_copy(k).start()
    table_copy = pltpu.make_async_copy(table.at[pl.ds(low, rows)], rows_table, sems.at[1])
    table_copy.start()
    kv_copies = [
        pltpu.make_async_copy(
            piece,
            kv.at[pl.ds(pl.multiple_of((sp_rank ^ d) * span, span), span)],
            sems.at[2],
        )
        for d, piece in enumerate(kv_pieces)
    ]
    for copy in kv_copies:
        copy.start()
    out_parts = out_w.shape[0]
    out_columns = out_w.shape[2]

    def out_copy(k):
        return pltpu.make_async_copy(
            w_out.at[:, pl.ds(pl.multiple_of(k * out_columns, out_columns), out_columns)],
            out_w.at[k],
            o_sems.at[k * o_sems.shape[0] // out_parts],
        )

    wait_for(held, sems.at[0])
    table_copy.wait()
    factor = HD ** (-0.5) * log2_e
    cos, sin = rows_table[:, :HD] * factor, rows_table[:, HD : 2 * HD] * factor
    pair = piece_columns // HD

    @pl.loop(0, parts)
    def _(k):
        query_copy(k).wait()

        @pl.when(k == 0)
        def _():
            for i in range(out_parts):
                out_copy(i).start()

        total = jnp.dot(held[...], query_w[k], preferred_element_type=jnp.float32)
        for h in range(pair):
            field = total[:, h * HD : (h + 1) * HD]
            swapped = pltpu.roll(field, HD // 2, 1)
            at = pl.multiple_of((k * pair + h) * rows, rows)
            query[pl.ds(at, rows), :] = (field * cos + swapped * sin).astype(jnp.bfloat16)

    wait_for(kv, sems.at[2])
    top[...] = jnp.full_like(top, masked_score)
    acc[...] = jnp.zeros_like(acc)
    first = rows_table[:, 2 * HD : 2 * HD + 1].astype(jnp.int32)
    row_index = base + low + lax.broadcasted_iota(jnp.int32, (rows, BLOCK), 0)
    column = lax.broadcasted_iota(jnp.int32, (rows, BLOCK), 1)
    ones = jnp.ones((BLOCK, HD), jnp.bfloat16)
    together = min(heads, GROUP)

    def step(j, carry):
        offset = pl.multiple_of(j * BLOCK, BLOCK)
        key_index = column + offset
        bias = jnp.where((key_index <= row_index) & (key_index >= first), 0.0, masked_score)
        key = kv[pl.ds(offset, BLOCK), :HD]
        value = jnp.concatenate([kv[pl.ds(offset, BLOCK), HD:], ones], axis=1)
        for g in range(heads // together):
            span = slice(g * together * rows, (g + 1) * together * rows)
            scores = lax.dot_general(
                query[span], key, (((1,), (1,)), ((), ())), preferred_element_type=jnp.float32
            )
            scores = (scores.reshape(together, rows, BLOCK) + bias[None]).reshape(-1, BLOCK)
            old = top[span]
            new = jnp.maximum(old, jnp.max(scores, axis=1, keepdims=True))
            exps = jnp.exp2(scores - new[:, :1]).astype(jnp.bfloat16)
            mixed = jnp.dot(exps, value, preferred_element_type=jnp.float32)
            keep = jnp.exp2(old - new)
            acc[span] = acc[span] * jnp.concatenate([keep, keep], axis=1) + mixed
            top[span] = new
        return carry

    lax.fori_loop(start, (base + low + rows - 1) // BLOCK + 1, step, 0)
    for h in range(heads):
        span = slice(h * rows, (h + 1) * rows)
        flat[:, h * HD : (h + 1) * HD] = (acc[span, :HD] / acc[span, HD:]).astype(jnp.bfloat16)

    per_block = width // out_columns

    @pl.loop(0, count)
    def _(b):
        for k in range(per_block):
            out_copy(b * per_block + k).wait()
            out[b, :, k * out_columns : (k + 1) * out_columns] = jnp.dot(
                flat[...], out_w[b * per_block + k], preferred_element_type=jnp.float32
            ).astype(jnp.bfloat16)


def chunk_terms(count, low, rows, scaled, arrived, info, w_query, w_out, table, kv_pieces):
    width = scaled.shape[1]
    model, columns = w_query.shape
    inner = w_out.shape[0]
    heads = columns // HD
    tokens = kv_pieces[0].shape[0] * len(kv_pieces)
    pieces = [scaled] + [piece for _, _, piece in arrived]
    pieces_of = [(kind, step) for kind, step, _ in arrived]
    q_columns = min(columns, 256)
    o_columns = min(width, 1024)
    q_parts, o_parts = columns // q_columns, model // o_columns
    return pl.pallas_call(
        functools.partial(chunk_kernel, count, pieces_of, low),
        out_shape=jax.ShapeDtypeStruct((count, rows, width), jnp.bfloat16),
        in_specs=[SMEM] + [ANY] * (len(pieces) + 3 + len(kv_pieces)),
        out_specs=VMEM,
        scratch_shapes=[
            pltpu.VMEM((rows, model), jnp.bfloat16),
            pltpu.VMEM((q_parts, model, q_columns), jnp.bfloat16),
            pltpu.VMEM((o_parts, inner, o_columns), jnp.bfloat16),
            pltpu.VMEM((rows, table.shape[1]), jnp.float32),
            pltpu.VMEM((tokens, 2 * HD), jnp.bfloat16),
            pltpu.VMEM((heads * rows, HD), jnp.bfloat16),
            pltpu.VMEM((heads * rows, HD), jnp.float32),
            pltpu.VMEM((heads * rows, 2 * HD), jnp.float32),
            pltpu.VMEM((rows, inner), jnp.bfloat16),
            pltpu.SemaphoreType.DMA((3,)),
            pltpu.SemaphoreType.DMA((q_parts,)),
            pltpu.SemaphoreType.DMA((o_parts,)),
        ],
        compiler_params=pltpu.CompilerParams(vmem_limit_bytes=VMEM_LIMIT),
        cost_estimate=pl.CostEstimate(flops=rows * model * columns, bytes_accessed=0, transcendentals=0),
        name="chunk_terms",
    )(info, *[in_hbm(x) for x in (*pieces, w_query, w_out, table, *kv_pieces)])


def kv_kernel(group, slots, info_ref, scaled, w_key, w_value, *refs):
    outs = refs[: len(slots)]
    held, key_w, value_w, key, value, sems = refs[len(slots) :]
    copies = [
        pltpu.make_async_copy(source, target, sems.at[k])
        for k, (source, target) in enumerate(((scaled, held), (w_key, key_w), (w_value, value_w)))
    ]
    for copy in copies:
        copy.start()
    copies[0].wait()
    copies[1].wait()
    key[...] = jnp.dot(held[...], key_w[...], preferred_element_type=jnp.float32).astype(jnp.bfloat16)
    copies[2].wait()
    value[...] = jnp.dot(held[...], value_w[...], preferred_element_type=jnp.float32).astype(jnp.bfloat16)
    width = outs[0].shape[-1]
    rows = key.shape[0] * 2 * HD // width
    for out, devices in zip(outs, slots):
        for n, device in enumerate(devices(info_ref[0])):
            columns = pl.ds(pl.multiple_of(device * info_ref[3] // group * HD, HD), HD)
            for i in range(width // (2 * HD)):
                at = i * 2 * HD
                span = slice(i * rows, (i + 1) * rows)
                out[n * rows : (n + 1) * rows, at : at + HD] = key[span, columns]
                out[n * rows : (n + 1) * rows, at + HD : at + 2 * HD] = value[span, columns]


def kv_terms_of(slots, info, scaled, w_key, w_value):
    rows, width = scaled.shape
    columns = w_key.shape[1]
    pack = rows * 2 * HD // width
    shapes = [
        jax.ShapeDtypeStruct((pack * len(devices(0)), width), jnp.bfloat16) for devices in slots
    ]
    return pl.pallas_call(
        functools.partial(kv_kernel, HQ // KV, slots),
        out_shape=shapes,
        in_specs=[SMEM] + [ANY] * 3,
        out_specs=[VMEM] * len(slots),
        scratch_shapes=[
            pltpu.VMEM((rows, width), jnp.bfloat16),
            pltpu.VMEM((width, columns), jnp.bfloat16),
            pltpu.VMEM((width, columns), jnp.bfloat16),
            pltpu.VMEM((rows, columns), jnp.bfloat16),
            pltpu.VMEM((rows, columns), jnp.bfloat16),
            pltpu.SemaphoreType.DMA((3,)),
        ],
        compiler_params=pltpu.CompilerParams(vmem_limit_bytes=VMEM_LIMIT),
        cost_estimate=pl.CostEstimate(flops=0, bytes_accessed=2 * rows * width, transcendentals=0),
        name="kv_terms",
    )(info, in_hbm(scaled), in_hbm(w_key), in_hbm(w_value))


def kv_total_kernel(packed, table, out):
    rows, width = packed.shape
    for i in range(width // (2 * HD)):
        at = i * 2 * HD
        span = slice(i * rows, (i + 1) * rows)
        key, value = packed[:, at : at + HD], packed[:, at + HD : at + 2 * HD]
        rotated = key * table[span, :HD] + pltpu.roll(key, HD // 2, 1) * table[span, HD : 2 * HD]
        out[span, :HD] = rotated.astype(jnp.bfloat16)
        out[span, HD:] = (value * table[span, 3 * HD :]).astype(jnp.bfloat16)


def kv_total(packed, table):
    return pl.pallas_call(
        kv_total_kernel,
        out_shape=jax.ShapeDtypeStruct((table.shape[0], 2 * HD), jnp.bfloat16),
        in_specs=[VMEM] * 2,
        out_specs=VMEM,
        compiler_params=pltpu.CompilerParams(vmem_limit_bytes=VMEM_LIMIT),
        cost_estimate=pl.CostEstimate(flops=0, bytes_accessed=8 * packed.size, transcendentals=0),
        name="kv_total",
    )(packed, table)


def finish_kernel(count, low, has_inner, info_ref, hidden, terms, outer, inner, *refs):
    out, a, b, c, d, total, sems = refs[-7:]
    rows = a.shape[0]
    rank = info_ref[0]
    copies = [
        pltpu.make_async_copy(source, target, sems.at[k])
        for k, (source, target) in enumerate(
            [(hidden.at[pl.ds(low, rows)], a), (terms.at[rank], b), (outer, c), (inner, d)]
        )
    ]
    for copy in copies:
        copy.start()
    for copy in copies:
        copy.wait()
    summed = b[...].astype(jnp.float32) + c[...].astype(jnp.float32)
    middle = (rank > 0) & (rank < count - 1)
    other = jnp.where(middle, d[...].astype(jnp.float32), 0.0)
    total[...] = (a[...].astype(jnp.float32) + (summed + other)).astype(jnp.bfloat16)
    copy = pltpu.make_async_copy(total, out.at[pl.ds(low, rows)], sems.at[4])
    copy.start()
    copy.wait()


def finish(count, low, info, hidden, terms, last, out):
    _, rows, width = terms.shape
    outer, inner = last
    operands = [info, hidden, terms, outer, inner if inner is not None else outer]
    aliases = {}
    if out is not None:
        aliases = {len(operands): 0}
        operands.append(out)
    return pl.pallas_call(
        functools.partial(finish_kernel, count, low, inner is not None),
        out_shape=jax.ShapeDtypeStruct(hidden.shape, jnp.bfloat16),
        in_specs=[SMEM] + [ANY] * (len(operands) - 1),
        out_specs=ANY,
        scratch_shapes=[pltpu.VMEM((rows, width), jnp.bfloat16)] * 5 + [pltpu.SemaphoreType.DMA((5,))],
        input_output_aliases=aliases,
        cost_estimate=pl.CostEstimate(flops=0, bytes_accessed=6 * rows * width, transcendentals=0),
        compiler_params=pltpu.CompilerParams(vmem_limit_bytes=VMEM_LIMIT),
        name="finish",
    )(*operands)


def after(value, others):
    return lax.optimization_barrier((value, others))[0]


def exchange_sum(value, axis, size):
    parts = [lax.ppermute(value, axis, [(i, i ^ d) for i in range(size)]) for d in range(1, size)]
    return sum(parts, value)


class Line:
    def __init__(self, count, sp_count, rank):
        self.count, self.rank = count, rank
        self.even = rank % 2 == 0
        self.middle = (rank > 0) & (rank < count - 1)
        self.outer_pairs = [(i, i ^ 1) for i in range(count)]
        self.inner_pairs = []
        for i in range(count):
            for s in range(sp_count):
                partner = i + 1 if i % 2 else i - 1
                if 0 < i < count - 1:
                    self.inner_pairs.append((i * sp_count + s, partner * sp_count + s))
                else:
                    self.inner_pairs.append((i * sp_count + s, i * sp_count + (s ^ 1)))

    def outer(self, value, step=None, gather=True):
        pairs = self.outer_pairs
        if step is not None and gather:
            pairs = [
                (i, p) for i, p in pairs if (i >= step - 1 if i % 2 == 0 else i <= self.count - step)
            ]
        elif step is not None:
            pairs = [
                (i, p) for i, p in pairs if (i <= step - 1 if i % 2 == 0 else i >= self.count - step)
            ]
        return lax.ppermute(value, "tp", pairs)

    def inner(self, value):
        return lax.ppermute(value, ("tp", "sp"), self.inner_pairs)

    def term(self, terms, upward, step):
        dest = jnp.where(upward, self.rank + self.count - step, self.rank - self.count + step)
        valid = (dest >= 0) & (dest < self.count)
        return lax.dynamic_index_in_dim(terms, jnp.clip(dest, 0, self.count - 1), 0, False), valid

    def round(self, step, own, terms, last, earlier):
        count = self.count
        from_outer, from_inner = last
        gather_outer = own is not None and step < count
        gather_inner = own is not None and step < count - 1
        scatter_outer = terms is not None and step > 1
        scatter_inner = terms is not None and step > 2
        to_outer = to_inner = None
        if gather_outer:
            to_outer = own if step == 1 else from_inner
        if gather_inner:
            to_inner = own if step == 1 else from_outer
        if scatter_outer:
            mine, valid = self.term(terms, self.even, step - 1)
            if step > 3:
                added = (mine.astype(jnp.float32) + from_inner.astype(jnp.float32)).astype(jnp.bfloat16)
                mine = jnp.where(self.middle, added, mine)
            to_outer = mine if to_outer is None else jnp.where(valid, mine, to_outer)
        if scatter_inner:
            mine, valid = self.term(terms, ~self.even, step - 1)
            mine = (mine.astype(jnp.float32) + from_outer.astype(jnp.float32)).astype(jnp.bfloat16)
            to_inner = mine if to_inner is None else jnp.where(valid, mine, to_inner)
        to_outer, to_inner = after((to_outer, to_inner), earlier)
        alone = step if terms is None and step > 1 else None
        got_outer = None if to_outer is None else self.outer(to_outer, alone)
        got_inner = None if to_inner is None else self.inner(to_inner)
        return got_outer, got_inner

    def scatter(self, terms, earlier):
        last = (None, None)
        for step in range(2, self.count + 1):
            last = self.round(step, None, terms, last, earlier)
        return self.total(terms, last)

    def add(self, a, b):
        return (a.astype(jnp.float32) + b.astype(jnp.float32)).astype(jnp.bfloat16)

    def total(self, terms, last):
        mine = lax.dynamic_index_in_dim(terms, self.rank, 0, False).astype(jnp.float32)
        mine = mine + last[0].astype(jnp.float32)
        return jnp.where(self.middle, mine + last[1].astype(jnp.float32), mine)


def make_body(count, sp_count):
    def body(hidden, doc_ids, gain, w_query, w_key, w_value, w_out):
        rows, width = hidden.shape
        rank = lax.axis_index("tp")
        sp_rank = lax.axis_index("sp")
        heads = w_query.shape[1] // HD
        group = HQ // KV
        model = width * count
        line = Line(count, sp_count, rank)
        gain_own = lax.dynamic_slice_in_dim(gain, rank * width, width, 0).astype(jnp.float32)
        hidden_f = hidden.astype(jnp.float32)
        scaled = (hidden_f * gain_own[None, :]).astype(jnp.bfloat16)
        squares = exchange_sum(jnp.sum(hidden_f * hidden_f, axis=1), "tp", count)
        chunk = rows // (PERIODS * STREAMS)

        labels = jnp.arange(DOCS, dtype=jnp.int32)
        starts = exchange_sum(
            jnp.sum((doc_ids[None, :] < labels[:, None]).astype(jnp.int32), axis=1), "sp", sp_count
        )
        pack = rows * 2 * HD // width
        packed = count == 4 and chunk == 2 * pack
        kv_info = jnp.stack([rank, rank, rank, jnp.int32(heads)]).astype(jnp.int32)
        if packed:
            ends, across, swap, kv_own = kv_terms_of(
                (
                    lambda r: (3 - r, jnp.where(r == 0, 2, 1)),
                    lambda r: (jnp.where(r == 1, 3, 0), jnp.where(r == 1, 2, 1)),
                    lambda r: (r ^ 1,),
                    lambda r: (r,),
                ),
                kv_info,
                after(scaled, squares),
                w_key,
                w_value,
            )
        else:
            (kv_terms,) = kv_terms_of((lambda r: tuple(range(count)),), kv_info, scaled, w_key, w_value)
            kv_terms = kv_terms.reshape(count, pack, width)

        def positions():
            base = sp_rank * rows
            own_index = base + jnp.arange(rows, dtype=jnp.int32)
            first = jnp.sum(
                jnp.where(doc_ids[:, None] == labels[None, :], starts[None, :], 0), axis=1
            )
            cosine, sine = rope_tables(own_index - first)
            inverse = lax.rsqrt(squares / model + norm_eps)[:, None]
            table = jnp.concatenate(
                [
                    cosine * inverse,
                    sine * inverse,
                    jnp.broadcast_to(first.astype(jnp.float32)[:, None], (rows, HD)),
                    jnp.broadcast_to(inverse, (rows, HD)),
                ],
                axis=1,
            )
            infos = [
                jnp.stack([rank, first[k * chunk] // BLOCK, sp_rank]).astype(jnp.int32)
                for k in range(PERIODS * STREAMS)
            ]
            return table, infos

        out = None
        kv_pieces = None
        last = [(None, None)] * STREAMS
        terms = [None] * STREAMS
        history = []
        for period in range(PERIODS + 1):
            gather = period < PERIODS
            owns = [None] * STREAMS
            arrived = [[] for _ in range(STREAMS)]
            for step in range(1, count + 1):
                for j in range(STREAMS):
                    if not (gather and step < count) and not (terms[j] is not None and step > 1):
                        continue
                    if gather and step == 1:
                        low = (period * STREAMS + j) * chunk
                        owns[j] = scaled[low : low + chunk]
                    earlier = [history[-STREAMS - 1 : -STREAMS], last[j]]

                    last[j] = line.round(step, owns[j], terms[j], last[j], earlier)
                    history.append(last[j])
                    if gather and step < count:
                        arrived[j].append(("outer", step, last[j][0]))
                        if step < count - 1:
                            arrived[j].append(("inner", step, last[j][1]))
                    if packed and period == 0 and j == STREAMS - 1 and step == 1:
                        met = line.outer(ends, 1, gather=False)
                        crossed = line.inner(after(line.add(across, met), last[j]))
                    if packed and period == 0 and j == STREAMS - 1 and step == 2:
                        mine = jnp.where(line.middle, line.add(swap, crossed[:pack]), swap)
                        met = line.outer(after(mine, last[j])).astype(jnp.float32)
                        kv = kv_own.astype(jnp.float32) + met
                        kv = jnp.where(line.middle, kv + crossed[pack:].astype(jnp.float32), kv)
            if period == 0:
                table, infos = positions()
                if not packed:
                    kv = line.scatter(kv_terms, history[-1])
                kv = kv_total(kv, table)
                kv_pieces = [kv] + [
                    lax.ppermute(kv, "sp", [(i, i ^ d) for i in range(sp_count)])
                    for d in range(1, sp_count)
                ]
            for j in range(STREAMS):
                if terms[j] is not None:
                    low = ((period - 1) * STREAMS + j) * chunk
                    out = finish(count, low, infos[0], hidden, terms[j], last[j], out)
                if gather:
                    k = period * STREAMS + j
                    terms[j] = chunk_terms(
                        count, k * chunk, chunk, scaled, arrived[j], infos[k], w_query, w_out, table, kv_pieces
                    )
        return out

    return body


def solution(mesh):
    placed = (
        P(("rep", "sp"), "tp"),
        P(("rep", "sp")),
        P(),
        P(None, "tp"),
        P("tp", None),
        P("tp", None),
        P("tp", None),
    )
    body = make_body(mesh.shape["tp"], mesh.shape["sp"])
    return jax.shard_map(
        body, mesh=mesh, in_specs=placed, out_specs=P(("rep", "sp"), "tp"), check_vma=False
    )
```

```python
import functools

import jax
import jax.numpy as jnp
from jax import lax
from jax.experimental import pallas as pl
from jax.experimental.pallas import tpu as pltpu
from jax.sharding import PartitionSpec as P

HD = 128
HQ = 32
KV = 4
DOCS = 4
PERIODS = 2
STREAMS = 2

rope_base = 500000.0
norm_eps = 1e-05
masked_score = -1e30
log2_e = 1.4426950408889634
VMEM_LIMIT = 52 * 1024 * 1024
GROUP = 2
BLOCK = 512
VMEM = pl.BlockSpec(memory_space=pltpu.VMEM)
SMEM = pl.BlockSpec(memory_space=pltpu.SMEM)
ANY = pl.BlockSpec(memory_space=pl.ANY)


def rope_tables(positions):
    half_dim = HD // 2
    steps_index = jnp.arange(half_dim, dtype=jnp.float32)
    frequency = jnp.power(rope_base, -2.0 * steps_index / HD)
    angles = positions.astype(jnp.float32)[:, None] * frequency[None, :]
    cosine, sine = jnp.cos(angles), jnp.sin(angles)
    return jnp.concatenate([cosine, cosine], axis=1), jnp.concatenate([-sine, sine], axis=1)


def rotate(field, cosine, sine):
    half_dim = HD // 2
    swapped = jnp.concatenate([field[..., half_dim:], field[..., :half_dim]], axis=-1)
    return field * cosine + swapped * sine


def in_hbm(value):
    return pltpu.with_memory_space_constraint(value, pltpu.HBM)


def wait_for(target, sem):
    pltpu.make_async_copy(target, target, sem).wait()


def chunk_kernel(count, pieces_of, low, info_ref, scaled, *refs):
    streams = len(pieces_of)
    kept = []
    for of in pieces_of:
        kept.append(refs[: len(of)])
        refs = refs[len(of) :]
    w_query, w_out, table = refs[:3]
    outs, refs = refs[-12 - streams : -12], refs[3 : -12 - streams] + refs[-12:]
    kv_pieces = refs[:-12]
    held, query_w, out_w, rows_table, kv, query, top, acc, flat, sems, q_sems, o_sems = refs[-12:]
    rows = held.shape[0]
    each = rows // streams
    width = held.shape[1] // count
    parts, depth, piece_columns = query_w.shape[0], query_w.shape[1], query_w.shape[2]
    heads = query.shape[0] // rows
    rank, start, sp_rank = info_ref[0], info_ref[1], info_ref[2]
    span = kv_pieces[0].shape[0]
    base = sp_rank * span
    even = rank % 2 == 0

    def place(source, first_row, count_rows, block):
        columns = pl.ds(pl.multiple_of(block * width, width), width)
        target = held.at[first_row : first_row + count_rows, columns]
        return pltpu.make_async_copy(source, target, sems.at[0])

    place(scaled.at[pl.ds(low, rows)], 0, rows, rank).start()
    for j in range(streams):
        for piece, (kind, step) in zip(kept[j], pieces_of[j]):
            block = jnp.where(even == (kind == "outer"), rank + step, rank - step)

            @pl.when((block >= 0) & (block < count))
            def _():
                place(piece, j * each, each, block).start()

    def query_copy(k):
        return pltpu.make_async_copy(
            w_query.at[:, pl.ds(pl.multiple_of(k * piece_columns, piece_columns), piece_columns)],
            query_w.at[k],
            q_sems.at[k * q_sems.shape[0] // parts],
        )

    for k in range(parts):
        query_copy(k).start()
    table_copy = pltpu.make_async_copy(table.at[pl.ds(low, rows)], rows_table, sems.at[1])
    table_copy.start()
    kv_copies = [
        pltpu.make_async_copy(
            piece,
            kv.at[pl.ds(pl.multiple_of((sp_rank ^ d) * span, span), span)],
            sems.at[2],
        )
        for d, piece in enumerate(kv_pieces)
    ]
    for copy in kv_copies:
        copy.start()
    out_parts = out_w.shape[0]
    out_columns = out_w.shape[2]

    def out_copy(k):
        return pltpu.make_async_copy(
            w_out.at[:, pl.ds(pl.multiple_of(k * out_columns, out_columns), out_columns)],
            out_w.at[k],
            o_sems.at[k * o_sems.shape[0] // out_parts],
        )

    wait_for(held, sems.at[0])
    table_copy.wait()
    factor = HD ** (-0.5) * log2_e
    cos, sin = rows_table[:, :HD] * factor, rows_table[:, HD : 2 * HD] * factor
    pair = piece_columns // HD

    @pl.loop(0, parts)
    def _(k):
        query_copy(k).wait()

        @pl.when(k == 0)
        def _():
            for i in range(out_parts):
                out_copy(i).start()

        total = jnp.dot(held[...], query_w[k], preferred_element_type=jnp.float32)
        for h in range(pair):
            field = total[:, h * HD : (h + 1) * HD]
            swapped = pltpu.roll(field, HD // 2, 1)
            at = pl.multiple_of((k * pair + h) * rows, rows)
            query[pl.ds(at, rows), :] = (field * cos + swapped * sin).astype(jnp.bfloat16)

    wait_for(kv, sems.at[2])
    top[...] = jnp.full_like(top, masked_score)
    acc[...] = jnp.zeros_like(acc)
    first = rows_table[:, 2 * HD : 2 * HD + 1].astype(jnp.int32)
    row_index = base + low + lax.broadcasted_iota(jnp.int32, (rows, BLOCK), 0)
    column = lax.broadcasted_iota(jnp.int32, (rows, BLOCK), 1)
    ones = jnp.ones((BLOCK, HD), jnp.bfloat16)
    together = min(heads, GROUP)

    def step(j, carry):
        offset = pl.multiple_of(j * BLOCK, BLOCK)
        key_index = column + offset
        bias = jnp.where((key_index <= row_index) & (key_index >= first), 0.0, masked_score)
        key = kv[pl.ds(offset, BLOCK), :HD]
        value = jnp.concatenate([kv[pl.ds(offset, BLOCK), HD:], ones], axis=1)
        for g in range(heads // together):
            span = slice(g * together * rows, (g + 1) * together * rows)
            scores = lax.dot_general(
                query[span], key, (((1,), (1,)), ((), ())), preferred_element_type=jnp.float32
            )
            scores = (scores.reshape(together, rows, BLOCK) + bias[None]).reshape(-1, BLOCK)
            old = top[span]
            new = jnp.maximum(old, jnp.max(scores, axis=1, keepdims=True))
            exps = jnp.exp2(scores - new[:, :1]).astype(jnp.bfloat16)
            mixed = jnp.dot(exps, value, preferred_element_type=jnp.float32)
            keep = jnp.exp2(old - new)
            acc[span] = acc[span] * jnp.concatenate([keep, keep], axis=1) + mixed
            top[span] = new
        return carry

    lax.fori_loop(start, (base + low + rows - 1) // BLOCK + 1, step, 0)
    for h in range(heads):
        span = slice(h * rows, (h + 1) * rows)
        flat[:, h * HD : (h + 1) * HD] = (acc[span, :HD] / acc[span, HD:]).astype(jnp.bfloat16)

    per_block = width // out_columns

    @pl.loop(0, count)
    def _(b):
        for k in range(per_block):
            out_copy(b * per_block + k).wait()
            mixed = jnp.dot(flat[...], out_w[b * per_block + k], preferred_element_type=jnp.float32)
            for j in range(streams):
                outs[j][b, :, k * out_columns : (k + 1) * out_columns] = mixed[
                    j * each : (j + 1) * each
                ].astype(jnp.bfloat16)


def chunk_terms(count, low, each, scaled, arrived, info, w_query, w_out, table, kv_pieces):
    rows = each * len(arrived)
    width = scaled.shape[1]
    model, columns = w_query.shape
    inner = w_out.shape[0]
    heads = columns // HD
    tokens = kv_pieces[0].shape[0] * len(kv_pieces)
    pieces = [scaled] + [piece for of in arrived for _, _, piece in of]
    pieces_of = [[(kind, step) for kind, step, _ in of] for of in arrived]
    q_columns = min(columns, 256)
    o_columns = min(width, 1024)
    q_parts, o_parts = columns // q_columns, model // o_columns
    return pl.pallas_call(
        functools.partial(chunk_kernel, count, pieces_of, low),
        out_shape=[jax.ShapeDtypeStruct((count, each, width), jnp.bfloat16)] * len(arrived),
        in_specs=[SMEM] + [ANY] * (len(pieces) + 3 + len(kv_pieces)),
        out_specs=[VMEM] * len(arrived),
        scratch_shapes=[
            pltpu.VMEM((rows, model), jnp.bfloat16),
            pltpu.VMEM((q_parts, model, q_columns), jnp.bfloat16),
            pltpu.VMEM((o_parts, inner, o_columns), jnp.bfloat16),
            pltpu.VMEM((rows, table.shape[1]), jnp.float32),
            pltpu.VMEM((tokens, 2 * HD), jnp.bfloat16),
            pltpu.VMEM((heads * rows, HD), jnp.bfloat16),
            pltpu.VMEM((heads * rows, HD), jnp.float32),
            pltpu.VMEM((heads * rows, 2 * HD), jnp.float32),
            pltpu.VMEM((rows, inner), jnp.bfloat16),
            pltpu.SemaphoreType.DMA((3,)),
            pltpu.SemaphoreType.DMA((q_parts,)),
            pltpu.SemaphoreType.DMA((o_parts,)),
        ],
        compiler_params=pltpu.CompilerParams(vmem_limit_bytes=VMEM_LIMIT),
        cost_estimate=pl.CostEstimate(flops=rows * model * columns, bytes_accessed=0, transcendentals=0),
        name="chunk_terms",
    )(info, *[in_hbm(x) for x in (*pieces, w_query, w_out, table, *kv_pieces)])


def kv_kernel(group, slots, info_ref, scaled, w_key, w_value, *refs):
    outs = refs[: len(slots)]
    held, key_w, value_w, key, value, sems = refs[len(slots) :]
    copies = [
        pltpu.make_async_copy(source, target, sems.at[k])
        for k, (source, target) in enumerate(((scaled, held), (w_key, key_w), (w_value, value_w)))
    ]
    for copy in copies:
        copy.start()
    copies[0].wait()
    copies[1].wait()
    key[...] = jnp.dot(held[...], key_w[...], preferred_element_type=jnp.float32).astype(jnp.bfloat16)
    copies[2].wait()
    value[...] = jnp.dot(held[...], value_w[...], preferred_element_type=jnp.float32).astype(jnp.bfloat16)
    width = outs[0].shape[-1]
    rows = key.shape[0] * 2 * HD // width
    for out, devices in zip(outs, slots):
        for n, device in enumerate(devices(info_ref[0])):
            columns = pl.ds(pl.multiple_of(device * info_ref[3] // group * HD, HD), HD)
            for i in range(width // (2 * HD)):
                at = i * 2 * HD
                span = slice(i * rows, (i + 1) * rows)
                out[n * rows : (n + 1) * rows, at : at + HD] = key[span, columns]
                out[n * rows : (n + 1) * rows, at + HD : at + 2 * HD] = value[span, columns]


def kv_terms_of(slots, info, scaled, w_key, w_value):
    rows, width = scaled.shape
    columns = w_key.shape[1]
    pack = rows * 2 * HD // width
    shapes = [
        jax.ShapeDtypeStruct((pack * len(devices(0)), width), jnp.bfloat16) for devices in slots
    ]
    return pl.pallas_call(
        functools.partial(kv_kernel, HQ // KV, slots),
        out_shape=shapes,
        in_specs=[SMEM] + [ANY] * 3,
        out_specs=[VMEM] * len(slots),
        scratch_shapes=[
            pltpu.VMEM((rows, width), jnp.bfloat16),
            pltpu.VMEM((width, columns), jnp.bfloat16),
            pltpu.VMEM((width, columns), jnp.bfloat16),
            pltpu.VMEM((rows, columns), jnp.bfloat16),
            pltpu.VMEM((rows, columns), jnp.bfloat16),
            pltpu.SemaphoreType.DMA((3,)),
        ],
        compiler_params=pltpu.CompilerParams(vmem_limit_bytes=VMEM_LIMIT),
        cost_estimate=pl.CostEstimate(flops=0, bytes_accessed=2 * rows * width, transcendentals=0),
        name="kv_terms",
    )(info, in_hbm(scaled), in_hbm(w_key), in_hbm(w_value))


def kv_total_kernel(packed, table, out):
    rows, width = packed.shape
    for i in range(width // (2 * HD)):
        at = i * 2 * HD
        span = slice(i * rows, (i + 1) * rows)
        key, value = packed[:, at : at + HD], packed[:, at + HD : at + 2 * HD]
        rotated = key * table[span, :HD] + pltpu.roll(key, HD // 2, 1) * table[span, HD : 2 * HD]
        out[span, :HD] = rotated.astype(jnp.bfloat16)
        out[span, HD:] = (value * table[span, 3 * HD :]).astype(jnp.bfloat16)


def kv_total(packed, table):
    return pl.pallas_call(
        kv_total_kernel,
        out_shape=jax.ShapeDtypeStruct((table.shape[0], 2 * HD), jnp.bfloat16),
        in_specs=[VMEM] * 2,
        out_specs=VMEM,
        compiler_params=pltpu.CompilerParams(vmem_limit_bytes=VMEM_LIMIT),
        cost_estimate=pl.CostEstimate(flops=0, bytes_accessed=8 * packed.size, transcendentals=0),
        name="kv_total",
    )(packed, table)


def finish_kernel(count, low, has_inner, info_ref, hidden, terms, outer, inner, *refs):
    out, a, b, c, d, total, sems = refs[-7:]
    rows = a.shape[0]
    rank = info_ref[0]
    copies = [
        pltpu.make_async_copy(source, target, sems.at[k])
        for k, (source, target) in enumerate(
            [(hidden.at[pl.ds(low, rows)], a), (terms.at[rank], b), (outer, c), (inner, d)]
        )
    ]
    for copy in copies:
        copy.start()
    for copy in copies:
        copy.wait()
    summed = b[...].astype(jnp.float32) + c[...].astype(jnp.float32)
    middle = (rank > 0) & (rank < count - 1)
    other = jnp.where(middle, d[...].astype(jnp.float32), 0.0)
    total[...] = (a[...].astype(jnp.float32) + (summed + other)).astype(jnp.bfloat16)
    copy = pltpu.make_async_copy(total, out.at[pl.ds(low, rows)], sems.at[4])
    copy.start()
    copy.wait()


def finish(count, low, info, hidden, terms, last, out):
    _, rows, width = terms.shape
    outer, inner = last
    operands = [info, hidden, terms, outer, inner if inner is not None else outer]
    aliases = {}
    if out is not None:
        aliases = {len(operands): 0}
        operands.append(out)
    return pl.pallas_call(
        functools.partial(finish_kernel, count, low, inner is not None),
        out_shape=jax.ShapeDtypeStruct(hidden.shape, jnp.bfloat16),
        in_specs=[SMEM] + [ANY] * (len(operands) - 1),
        out_specs=ANY,
        scratch_shapes=[pltpu.VMEM((rows, width), jnp.bfloat16)] * 5 + [pltpu.SemaphoreType.DMA((5,))],
        input_output_aliases=aliases,
        cost_estimate=pl.CostEstimate(flops=0, bytes_accessed=6 * rows * width, transcendentals=0),
        compiler_params=pltpu.CompilerParams(vmem_limit_bytes=VMEM_LIMIT),
        name="finish",
    )(*operands)


def after(value, others):
    return lax.optimization_barrier((value, others))[0]


def exchange_sum(value, axis, size):
    parts = [lax.ppermute(value, axis, [(i, i ^ d) for i in range(size)]) for d in range(1, size)]
    return sum(parts, value)


class Line:
    def __init__(self, count, sp_count, rank):
        self.count, self.rank = count, rank
        self.even = rank % 2 == 0
        self.middle = (rank > 0) & (rank < count - 1)
        self.outer_pairs = [(i, i ^ 1) for i in range(count)]
        self.inner_pairs = []
        for i in range(count):
            for s in range(sp_count):
                partner = i + 1 if i % 2 else i - 1
                if 0 < i < count - 1:
                    self.inner_pairs.append((i * sp_count + s, partner * sp_count + s))
                else:
                    self.inner_pairs.append((i * sp_count + s, i * sp_count + (s ^ 1)))

    def outer(self, value, step=None, gather=True):
        pairs = self.outer_pairs
        if step is not None and gather:
            pairs = [
                (i, p) for i, p in pairs if (i >= step - 1 if i % 2 == 0 else i <= self.count - step)
            ]
        elif step is not None:
            pairs = [
                (i, p) for i, p in pairs if (i <= step - 1 if i % 2 == 0 else i >= self.count - step)
            ]
        return lax.ppermute(value, "tp", pairs)

    def inner(self, value):
        return lax.ppermute(value, ("tp", "sp"), self.inner_pairs)

    def term(self, terms, upward, step):
        dest = jnp.where(upward, self.rank + self.count - step, self.rank - self.count + step)
        valid = (dest >= 0) & (dest < self.count)
        return lax.dynamic_index_in_dim(terms, jnp.clip(dest, 0, self.count - 1), 0, False), valid

    def round(self, step, own, terms, last, earlier):
        count = self.count
        from_outer, from_inner = last
        gather_outer = own is not None and step < count
        gather_inner = own is not None and step < count - 1
        scatter_outer = terms is not None and step > 1
        scatter_inner = terms is not None and step > 2
        to_outer = to_inner = None
        if gather_outer:
            to_outer = own if step == 1 else from_inner
        if gather_inner:
            to_inner = own if step == 1 else from_outer
        if scatter_outer:
            mine, valid = self.term(terms, self.even, step - 1)
            if step > 3:
                added = (mine.astype(jnp.float32) + from_inner.astype(jnp.float32)).astype(jnp.bfloat16)
                mine = jnp.where(self.middle, added, mine)
            to_outer = mine if to_outer is None else jnp.where(valid, mine, to_outer)
        if scatter_inner:
            mine, valid = self.term(terms, ~self.even, step - 1)
            mine = (mine.astype(jnp.float32) + from_outer.astype(jnp.float32)).astype(jnp.bfloat16)
            to_inner = mine if to_inner is None else jnp.where(valid, mine, to_inner)
        to_outer, to_inner = after((to_outer, to_inner), earlier)
        alone = step if terms is None and step > 1 else None
        got_outer = None if to_outer is None else self.outer(to_outer, alone)
        got_inner = None if to_inner is None else self.inner(to_inner)
        return got_outer, got_inner

    def scatter(self, terms, earlier):
        last = (None, None)
        for step in range(2, self.count + 1):
            last = self.round(step, None, terms, last, earlier)
        return self.total(terms, last)

    def add(self, a, b):
        return (a.astype(jnp.float32) + b.astype(jnp.float32)).astype(jnp.bfloat16)

    def total(self, terms, last):
        mine = lax.dynamic_index_in_dim(terms, self.rank, 0, False).astype(jnp.float32)
        mine = mine + last[0].astype(jnp.float32)
        return jnp.where(self.middle, mine + last[1].astype(jnp.float32), mine)


def make_body(count, sp_count):
    def body(hidden, doc_ids, gain, w_query, w_key, w_value, w_out):
        rows, width = hidden.shape
        rank = lax.axis_index("tp")
        sp_rank = lax.axis_index("sp")
        heads = w_query.shape[1] // HD
        group = HQ // KV
        model = width * count
        line = Line(count, sp_count, rank)
        gain_own = lax.dynamic_slice_in_dim(gain, rank * width, width, 0).astype(jnp.float32)
        hidden_f = hidden.astype(jnp.float32)
        scaled = (hidden_f * gain_own[None, :]).astype(jnp.bfloat16)
        squares = exchange_sum(jnp.sum(hidden_f * hidden_f, axis=1), "tp", count)
        chunk = rows // (PERIODS * STREAMS)

        labels = jnp.arange(DOCS, dtype=jnp.int32)
        starts = exchange_sum(
            jnp.sum((doc_ids[None, :] < labels[:, None]).astype(jnp.int32), axis=1), "sp", sp_count
        )
        pack = rows * 2 * HD // width
        packed = count == 4 and chunk == 2 * pack
        kv_info = jnp.stack([rank, rank, rank, jnp.int32(heads)]).astype(jnp.int32)
        if packed:
            ends, across, swap, kv_own = kv_terms_of(
                (
                    lambda r: (3 - r, jnp.where(r == 0, 2, 1)),
                    lambda r: (jnp.where(r == 1, 3, 0), jnp.where(r == 1, 2, 1)),
                    lambda r: (r ^ 1,),
                    lambda r: (r,),
                ),
                kv_info,
                after(scaled, squares),
                w_key,
                w_value,
            )
        else:
            (kv_terms,) = kv_terms_of((lambda r: tuple(range(count)),), kv_info, scaled, w_key, w_value)
            kv_terms = kv_terms.reshape(count, pack, width)

        def positions():
            base = sp_rank * rows
            own_index = base + jnp.arange(rows, dtype=jnp.int32)
            first = jnp.sum(
                jnp.where(doc_ids[:, None] == labels[None, :], starts[None, :], 0), axis=1
            )
            cosine, sine = rope_tables(own_index - first)
            inverse = lax.rsqrt(squares / model + norm_eps)[:, None]
            table = jnp.concatenate(
                [
                    cosine * inverse,
                    sine * inverse,
                    jnp.broadcast_to(first.astype(jnp.float32)[:, None], (rows, HD)),
                    jnp.broadcast_to(inverse, (rows, HD)),
                ],
                axis=1,
            )
            infos = [
                jnp.stack([rank, first[k * STREAMS * chunk] // BLOCK, sp_rank]).astype(jnp.int32)
                for k in range(PERIODS)
            ]
            return table, infos

        out = None
        kv_pieces = None
        last = [(None, None)] * STREAMS
        terms = [None] * STREAMS
        history = []
        for period in range(PERIODS + 1):
            gather = period < PERIODS
            owns = [None] * STREAMS
            arrived = [[] for _ in range(STREAMS)]
            for step in range(1, count + 1):
                for j in range(STREAMS):
                    if not (gather and step < count) and not (terms[j] is not None and step > 1):
                        continue
                    if gather and step == 1:
                        low = (period * STREAMS + j) * chunk
                        owns[j] = scaled[low : low + chunk]
                    earlier = [history[-STREAMS - 1 : -STREAMS], last[j]]

                    last[j] = line.round(step, owns[j], terms[j], last[j], earlier)
                    history.append(last[j])
                    if gather and step < count:
                        arrived[j].append(("outer", step, last[j][0]))
                        if step < count - 1:
                            arrived[j].append(("inner", step, last[j][1]))
                    if packed and period == 0 and j == STREAMS - 1 and step == 1:
                        met = line.outer(ends, 1, gather=False)
                        crossed = line.inner(after(line.add(across, met), last[j]))
                    if packed and period == 0 and j == STREAMS - 1 and step == 2:
                        mine = jnp.where(line.middle, line.add(swap, crossed[:pack]), swap)
                        met = line.outer(after(mine, last[j])).astype(jnp.float32)
                        kv = kv_own.astype(jnp.float32) + met
                        kv = jnp.where(line.middle, kv + crossed[pack:].astype(jnp.float32), kv)
            if period == 0:
                table, infos = positions()
                if not packed:
                    kv = line.scatter(kv_terms, history[-1])
                kv = kv_total(kv, table)
                kv_pieces = [kv] + [
                    lax.ppermute(kv, "sp", [(i, i ^ d) for i in range(sp_count)])
                    for d in range(1, sp_count)
                ]
            for j in range(STREAMS):
                if terms[j] is not None:
                    low = ((period - 1) * STREAMS + j) * chunk
                    out = finish(count, low, infos[0], hidden, terms[j], last[j], out)
            if gather:
                low = period * STREAMS * chunk
                terms = chunk_terms(
                    count, low, chunk, scaled, arrived, infos[period], w_query, w_out, table, kv_pieces
                )
        return out

    return body


def solution(mesh):
    placed = (
        P(("rep", "sp"), "tp"),
        P(("rep", "sp")),
        P(),
        P(None, "tp"),
        P("tp", None),
        P("tp", None),
        P("tp", None),
    )
    body = make_body(mesh.shape["tp"], mesh.shape["sp"])
    return jax.shard_map(
        body, mesh=mesh, in_specs=placed, out_specs=P(("rep", "sp"), "tp"), check_vma=False
    )
```

```python
import functools

import jax
import jax.numpy as jnp
from jax import lax
from jax.experimental import pallas as pl
from jax.experimental.pallas import tpu as pltpu
from jax.sharding import PartitionSpec as P

HD = 128
HQ = 32
KV = 4
DOCS = 4
PERIODS = 2
STREAMS = 2

rope_base = 500000.0
norm_eps = 1e-05
masked_score = -1e30
log2_e = 1.4426950408889634
VMEM_LIMIT = 42 * 1024 * 1024
GROUP = 2
BLOCK = 512
VMEM = pl.BlockSpec(memory_space=pltpu.VMEM)
SMEM = pl.BlockSpec(memory_space=pltpu.SMEM)
ANY = pl.BlockSpec(memory_space=pl.ANY)


def rope_tables(positions):
    half_dim = HD // 2
    steps_index = jnp.arange(half_dim, dtype=jnp.float32)
    frequency = jnp.power(rope_base, -2.0 * steps_index / HD)
    angles = positions.astype(jnp.float32)[:, None] * frequency[None, :]
    cosine, sine = jnp.cos(angles), jnp.sin(angles)
    return jnp.concatenate([cosine, cosine], axis=1), jnp.concatenate([-sine, sine], axis=1)


def rotate(field, cosine, sine):
    half_dim = HD // 2
    swapped = jnp.concatenate([field[..., half_dim:], field[..., :half_dim]], axis=-1)
    return field * cosine + swapped * sine


def in_hbm(value):
    return pltpu.with_memory_space_constraint(value, pltpu.HBM)


def wait_for(target, sem):
    pltpu.make_async_copy(target, target, sem).wait()


def chunk_kernel(count, pieces_of, low, info_ref, scaled, *refs):
    streams = len(pieces_of)
    kept = []
    for of in pieces_of:
        kept.append(refs[: len(of)])
        refs = refs[len(of) :]
    w_query, w_out, table = refs[:3]
    outs, refs = refs[-12 - streams : -12], refs[3 : -12 - streams] + refs[-12:]
    kv_pieces = refs[:-12]
    flat, held, query_w, out_w, rows_table, kv, query, top, acc, sems, q_sems, o_sems = refs[-12:]
    rows = held.shape[0]
    each = rows // streams
    width = held.shape[1] // count
    parts, depth, piece_columns = query_w.shape[0], query_w.shape[1], query_w.shape[2]
    heads = query.shape[0] // rows
    rank, start, sp_rank = info_ref[0], info_ref[1], info_ref[2]
    span = kv_pieces[0].shape[0]
    base = sp_rank * span
    even = rank % 2 == 0

    def place(source, first_row, count_rows, block):
        columns = pl.ds(pl.multiple_of(block * width, width), width)
        target = held.at[first_row : first_row + count_rows, columns]
        return pltpu.make_async_copy(source, target, sems.at[0])

    place(scaled.at[pl.ds(low, rows)], 0, rows, rank).start()
    for j in range(streams):
        for piece, (kind, step) in zip(kept[j], pieces_of[j]):
            block = jnp.where(even == (kind == "outer"), rank + step, rank - step)

            @pl.when((block >= 0) & (block < count))
            def _():
                place(piece, j * each, each, block).start()

    def query_copy(k):
        return pltpu.make_async_copy(
            w_query.at[:, pl.ds(pl.multiple_of(k * piece_columns, piece_columns), piece_columns)],
            query_w.at[k],
            q_sems.at[k * q_sems.shape[0] // parts],
        )

    for k in range(parts):
        query_copy(k).start()
    table_copy = pltpu.make_async_copy(table.at[pl.ds(low, rows)], rows_table, sems.at[1])
    table_copy.start()
    kv_copies = [
        pltpu.make_async_copy(
            piece,
            kv.at[pl.ds(pl.multiple_of((sp_rank ^ d) * span, span), span)],
            sems.at[2],
        )
        for d, piece in enumerate(kv_pieces)
    ]
    for copy in kv_copies:
        copy.start()
    out_parts = out_w.shape[0]
    out_columns = out_w.shape[2]
    far = jnp.where(rank < count // 2, count - 1, 0)

    def out_copy(k):
        at = pl.multiple_of(far * width + k * out_columns, out_columns)
        return pltpu.make_async_copy(w_out.at[:, pl.ds(at, out_columns)], out_w.at[k], o_sems.at[k])

    wait_for(held, sems.at[0])
    table_copy.wait()
    factor = HD ** (-0.5) * log2_e
    cos, sin = rows_table[:, :HD] * factor, rows_table[:, HD : 2 * HD] * factor
    pair = piece_columns // HD

    @pl.loop(0, parts)
    def _(k):
        query_copy(k).wait()

        @pl.when(k == 0)
        def _():
            for i in range(out_parts):
                out_copy(i).start()

        total = jnp.dot(held[...], query_w[k], preferred_element_type=jnp.float32)
        for h in range(pair):
            field = total[:, h * HD : (h + 1) * HD]
            swapped = pltpu.roll(field, HD // 2, 1)
            at = pl.multiple_of((k * pair + h) * rows, rows)
            query[pl.ds(at, rows), :] = (field * cos + swapped * sin).astype(jnp.bfloat16)

    wait_for(kv, sems.at[2])
    top[...] = jnp.full_like(top, masked_score)
    acc[...] = jnp.zeros_like(acc)
    first = rows_table[:, 2 * HD : 2 * HD + 1].astype(jnp.int32)
    row_index = base + low + lax.broadcasted_iota(jnp.int32, (rows, BLOCK), 0)
    column = lax.broadcasted_iota(jnp.int32, (rows, BLOCK), 1)
    ones = jnp.ones((BLOCK, HD), jnp.bfloat16)
    together = min(heads, GROUP)

    def step(j, carry):
        offset = pl.multiple_of(j * BLOCK, BLOCK)
        key_index = column + offset
        bias = jnp.where((key_index <= row_index) & (key_index >= first), 0.0, masked_score)
        key = kv[pl.ds(offset, BLOCK), :HD]
        value = jnp.concatenate([kv[pl.ds(offset, BLOCK), HD:], ones], axis=1)
        for g in range(heads // together):
            span = slice(g * together * rows, (g + 1) * together * rows)
            scores = lax.dot_general(
                query[span], key, (((1,), (1,)), ((), ())), preferred_element_type=jnp.float32
            )
            scores = (scores.reshape(together, rows, BLOCK) + bias[None]).reshape(-1, BLOCK)
            old = top[span]
            new = jnp.maximum(old, jnp.max(scores, axis=1, keepdims=True))
            exps = jnp.exp2(scores - new[:, :1]).astype(jnp.bfloat16)
            mixed = jnp.dot(exps, value, preferred_element_type=jnp.float32)
            keep = jnp.exp2(old - new)
            acc[span] = acc[span] * jnp.concatenate([keep, keep], axis=1) + mixed
            top[span] = new
        return carry

    lax.fori_loop(start, (base + low + rows - 1) // BLOCK + 1, step, 0)
    for h in range(heads):
        span = slice(h * rows, (h + 1) * rows)
        flat[:, h * HD : (h + 1) * HD] = (acc[span, :HD] / acc[span, HD:]).astype(jnp.bfloat16)

    for k in range(out_parts):
        out_copy(k).wait()
        mixed = jnp.dot(flat[...], out_w[k], preferred_element_type=jnp.float32)
        for j in range(streams):
            outs[j][:, k * out_columns : (k + 1) * out_columns] = mixed[
                j * each : (j + 1) * each
            ].astype(jnp.bfloat16)


def output_kernel(flat, w_out, *refs):
    outs, weight, sems = refs[:-2], refs[-2], refs[-1]
    count, each, width = outs[0].shape
    parts, _, columns = weight.shape
    per_block = parts // count

    def copy(k):
        at = pl.multiple_of(k * columns, columns)
        return pltpu.make_async_copy(w_out.at[:, pl.ds(at, columns)], weight.at[k], sems.at[k])

    for k in range(parts):
        copy(k).start()

    @pl.loop(0, count)
    def _(b):
        for k in range(per_block):
            copy(b * per_block + k).wait()
            mixed = jnp.dot(flat[...], weight[b * per_block + k], preferred_element_type=jnp.float32)
            for j, out in enumerate(outs):
                out[b, :, k * columns : (k + 1) * columns] = mixed[j * each : (j + 1) * each].astype(
                    jnp.bfloat16
                )


def output_terms(count, streams, flat, w_out):
    rows, inner = flat.shape
    width = w_out.shape[1] // count
    columns = min(width, 1024)
    parts = w_out.shape[1] // columns
    return pl.pallas_call(
        output_kernel,
        out_shape=[jax.ShapeDtypeStruct((count, rows // streams, width), jnp.bfloat16)] * streams,
        in_specs=[VMEM, ANY],
        out_specs=[VMEM] * streams,
        scratch_shapes=[
            pltpu.VMEM((parts, inner, columns), jnp.bfloat16),
            pltpu.SemaphoreType.DMA((parts,)),
        ],
        compiler_params=pltpu.CompilerParams(vmem_limit_bytes=VMEM_LIMIT),
        cost_estimate=pl.CostEstimate(
            flops=rows * inner * width * count, bytes_accessed=0, transcendentals=0
        ),
        name="output_terms",
    )(flat, in_hbm(w_out))


def chunk_terms(count, low, each, scaled, arrived, info, w_query, w_out, table, kv_pieces):
    rows = each * len(arrived)
    width = scaled.shape[1]
    model, columns = w_query.shape
    inner = w_out.shape[0]
    heads = columns // HD
    tokens = kv_pieces[0].shape[0] * len(kv_pieces)
    pieces = [scaled] + [piece for of in arrived for _, _, piece in of]
    pieces_of = [[(kind, step) for kind, step, _ in of] for of in arrived]
    q_columns = min(columns, 256)
    o_columns = min(width, 1024)
    q_parts, o_parts = columns // q_columns, width // o_columns
    return pl.pallas_call(
        functools.partial(chunk_kernel, count, pieces_of, low),
        out_shape=[jax.ShapeDtypeStruct((each, width), jnp.bfloat16)] * len(arrived)
        + [jax.ShapeDtypeStruct((rows, inner), jnp.bfloat16)],
        in_specs=[SMEM] + [ANY] * (len(pieces) + 3 + len(kv_pieces)),
        out_specs=[VMEM] * (len(arrived) + 1),
        scratch_shapes=[
            pltpu.VMEM((rows, model), jnp.bfloat16),
            pltpu.VMEM((q_parts, model, q_columns), jnp.bfloat16),
            pltpu.VMEM((o_parts, inner, o_columns), jnp.bfloat16),
            pltpu.VMEM((rows, table.shape[1]), jnp.float32),
            pltpu.VMEM((tokens, 2 * HD), jnp.bfloat16),
            pltpu.VMEM((heads * rows, HD), jnp.bfloat16),
            pltpu.VMEM((heads * rows, HD), jnp.float32),
            pltpu.VMEM((heads * rows, 2 * HD), jnp.float32),
            pltpu.SemaphoreType.DMA((3,)),
            pltpu.SemaphoreType.DMA((q_parts,)),
            pltpu.SemaphoreType.DMA((o_parts,)),
        ],
        compiler_params=pltpu.CompilerParams(vmem_limit_bytes=VMEM_LIMIT),
        cost_estimate=pl.CostEstimate(flops=rows * model * columns, bytes_accessed=0, transcendentals=0),
        name="chunk_terms",
    )(info, *[in_hbm(x) for x in (*pieces, w_query, w_out, table, *kv_pieces)])


def kv_kernel(group, slots, info_ref, scaled, w_key, w_value, *refs):
    outs = refs[: len(slots)]
    held, key_w, value_w, key, value, sems = refs[len(slots) :]
    copies = [
        pltpu.make_async_copy(source, target, sems.at[k])
        for k, (source, target) in enumerate(((scaled, held), (w_key, key_w), (w_value, value_w)))
    ]
    for copy in copies:
        copy.start()
    copies[0].wait()
    copies[1].wait()
    key[...] = jnp.dot(held[...], key_w[...], preferred_element_type=jnp.float32).astype(jnp.bfloat16)
    copies[2].wait()
    value[...] = jnp.dot(held[...], value_w[...], preferred_element_type=jnp.float32).astype(jnp.bfloat16)
    width = outs[0].shape[-1]
    rows = key.shape[0] * 2 * HD // width
    for out, devices in zip(outs, slots):
        for n, device in enumerate(devices(info_ref[0])):
            columns = pl.ds(pl.multiple_of(device * info_ref[3] // group * HD, HD), HD)
            for i in range(width // (2 * HD)):
                at = i * 2 * HD
                span = slice(i * rows, (i + 1) * rows)
                out[n * rows : (n + 1) * rows, at : at + HD] = key[span, columns]
                out[n * rows : (n + 1) * rows, at + HD : at + 2 * HD] = value[span, columns]


def kv_terms_of(slots, info, scaled, w_key, w_value):
    rows, width = scaled.shape
    columns = w_key.shape[1]
    pack = rows * 2 * HD // width
    shapes = [
        jax.ShapeDtypeStruct((pack * len(devices(0)), width), jnp.bfloat16) for devices in slots
    ]
    return pl.pallas_call(
        functools.partial(kv_kernel, HQ // KV, slots),
        out_shape=shapes,
        in_specs=[SMEM] + [ANY] * 3,
        out_specs=[VMEM] * len(slots),
        scratch_shapes=[
            pltpu.VMEM((rows, width), jnp.bfloat16),
            pltpu.VMEM((width, columns), jnp.bfloat16),
            pltpu.VMEM((width, columns), jnp.bfloat16),
            pltpu.VMEM((rows, columns), jnp.bfloat16),
            pltpu.VMEM((rows, columns), jnp.bfloat16),
            pltpu.SemaphoreType.DMA((3,)),
        ],
        compiler_params=pltpu.CompilerParams(vmem_limit_bytes=VMEM_LIMIT),
        cost_estimate=pl.CostEstimate(flops=0, bytes_accessed=2 * rows * width, transcendentals=0),
        name="kv_terms",
    )(info, in_hbm(scaled), in_hbm(w_key), in_hbm(w_value))


def kv_total_kernel(packed, table, out):
    rows, width = packed.shape
    for i in range(width // (2 * HD)):
        at = i * 2 * HD
        span = slice(i * rows, (i + 1) * rows)
        key, value = packed[:, at : at + HD], packed[:, at + HD : at + 2 * HD]
        rotated = key * table[span, :HD] + pltpu.roll(key, HD // 2, 1) * table[span, HD : 2 * HD]
        out[span, :HD] = rotated.astype(jnp.bfloat16)
        out[span, HD:] = (value * table[span, 3 * HD :]).astype(jnp.bfloat16)


def kv_total(packed, table):
    return pl.pallas_call(
        kv_total_kernel,
        out_shape=jax.ShapeDtypeStruct((table.shape[0], 2 * HD), jnp.bfloat16),
        in_specs=[VMEM] * 2,
        out_specs=VMEM,
        compiler_params=pltpu.CompilerParams(vmem_limit_bytes=VMEM_LIMIT),
        cost_estimate=pl.CostEstimate(flops=0, bytes_accessed=8 * packed.size, transcendentals=0),
        name="kv_total",
    )(packed, table)


def finish_kernel(count, low, has_inner, info_ref, hidden, terms, outer, inner, *refs):
    out, a, b, c, d, total, sems = refs[-7:]
    rows = a.shape[0]
    rank = info_ref[0]
    copies = [
        pltpu.make_async_copy(source, target, sems.at[k])
        for k, (source, target) in enumerate(
            [(hidden.at[pl.ds(low, rows)], a), (terms.at[rank], b), (outer, c), (inner, d)]
        )
    ]
    for copy in copies:
        copy.start()
    for copy in copies:
        copy.wait()
    summed = b[...].astype(jnp.float32) + c[...].astype(jnp.float32)
    middle = (rank > 0) & (rank < count - 1)
    other = jnp.where(middle, d[...].astype(jnp.float32), 0.0)
    total[...] = (a[...].astype(jnp.float32) + (summed + other)).astype(jnp.bfloat16)
    copy = pltpu.make_async_copy(total, out.at[pl.ds(low, rows)], sems.at[4])
    copy.start()
    copy.wait()


def finish(count, low, info, hidden, terms, last, out):
    _, rows, width = terms.shape
    outer, inner = last
    operands = [info, hidden, terms, outer, inner if inner is not None else outer]
    aliases = {}
    if out is not None:
        aliases = {len(operands): 0}
        operands.append(out)
    return pl.pallas_call(
        functools.partial(finish_kernel, count, low, inner is not None),
        out_shape=jax.ShapeDtypeStruct(hidden.shape, jnp.bfloat16),
        in_specs=[SMEM] + [ANY] * (len(operands) - 1),
        out_specs=ANY,
        scratch_shapes=[pltpu.VMEM((rows, width), jnp.bfloat16)] * 5 + [pltpu.SemaphoreType.DMA((5,))],
        input_output_aliases=aliases,
        cost_estimate=pl.CostEstimate(flops=0, bytes_accessed=6 * rows * width, transcendentals=0),
        compiler_params=pltpu.CompilerParams(vmem_limit_bytes=VMEM_LIMIT),
        name="finish",
    )(*operands)


def after(value, others):
    return lax.optimization_barrier((value, others))[0]


def exchange_sum(value, axis, size):
    parts = [lax.ppermute(value, axis, [(i, i ^ d) for i in range(size)]) for d in range(1, size)]
    return sum(parts, value)


class Line:
    def __init__(self, count, sp_count, rank):
        self.count, self.rank = count, rank
        self.even = rank % 2 == 0
        self.middle = (rank > 0) & (rank < count - 1)
        self.outer_pairs = [(i, i ^ 1) for i in range(count)]
        self.inner_pairs = []
        for i in range(count):
            for s in range(sp_count):
                partner = i + 1 if i % 2 else i - 1
                if 0 < i < count - 1:
                    self.inner_pairs.append((i * sp_count + s, partner * sp_count + s))
                else:
                    self.inner_pairs.append((i * sp_count + s, i * sp_count + (s ^ 1)))

    def outer(self, value, step=None, gather=True):
        pairs = self.outer_pairs
        if step is not None and gather:
            pairs = [
                (i, p) for i, p in pairs if (i >= step - 1 if i % 2 == 0 else i <= self.count - step)
            ]
        elif step is not None:
            pairs = [
                (i, p) for i, p in pairs if (i <= step - 1 if i % 2 == 0 else i >= self.count - step)
            ]
        return lax.ppermute(value, "tp", pairs)

    def inner(self, value):
        return lax.ppermute(value, ("tp", "sp"), self.inner_pairs)

    def term(self, terms, upward, step):
        dest = jnp.where(upward, self.rank + self.count - step, self.rank - self.count + step)
        valid = (dest >= 0) & (dest < self.count)
        if terms is None:
            return None, valid
        return lax.dynamic_index_in_dim(terms, jnp.clip(dest, 0, self.count - 1), 0, False), valid

    def round(self, step, own, terms, first, last, earlier):
        count = self.count
        from_outer, from_inner = last
        gather_outer = own is not None and step < count
        gather_inner = own is not None and step < count - 1
        scatter_outer = first is not None and step > 1
        scatter_inner = first is not None and step > 2
        to_outer = to_inner = None
        if gather_outer:
            to_outer = own if step == 1 else from_inner
        if gather_inner:
            to_inner = own if step == 1 else from_outer
        if scatter_outer:
            mine, valid = self.term(terms, self.even, step - 1)
            if step == 2:
                mine = first
            if step > 3:
                added = (mine.astype(jnp.float32) + from_inner.astype(jnp.float32)).astype(jnp.bfloat16)
                mine = jnp.where(self.middle, added, mine)
            to_outer = mine if to_outer is None else jnp.where(valid, mine, to_outer)
        if scatter_inner:
            mine, valid = self.term(terms, ~self.even, step - 1)
            mine = (mine.astype(jnp.float32) + from_outer.astype(jnp.float32)).astype(jnp.bfloat16)
            to_inner = mine if to_inner is None else jnp.where(valid, mine, to_inner)
        to_outer, to_inner = after((to_outer, to_inner), earlier)
        alone = step if first is None and step > 1 else None
        got_outer = None if to_outer is None else self.outer(to_outer, alone)
        got_inner = None if to_inner is None else self.inner(to_inner)
        return got_outer, got_inner

    def scatter(self, terms, earlier):
        last = (None, None)
        for step in range(2, self.count + 1):
            last = self.round(step, None, terms, self.term(terms, self.even, 1)[0], last, earlier)
        return self.total(terms, last)

    def add(self, a, b):
        return (a.astype(jnp.float32) + b.astype(jnp.float32)).astype(jnp.bfloat16)

    def total(self, terms, last):
        mine = lax.dynamic_index_in_dim(terms, self.rank, 0, False).astype(jnp.float32)
        mine = mine + last[0].astype(jnp.float32)
        return jnp.where(self.middle, mine + last[1].astype(jnp.float32), mine)


def make_body(count, sp_count):
    def body(hidden, doc_ids, gain, w_query, w_key, w_value, w_out):
        rows, width = hidden.shape
        rank = lax.axis_index("tp")
        sp_rank = lax.axis_index("sp")
        heads = w_query.shape[1] // HD
        group = HQ // KV
        model = width * count
        line = Line(count, sp_count, rank)
        gain_own = lax.dynamic_slice_in_dim(gain, rank * width, width, 0).astype(jnp.float32)
        hidden_f = hidden.astype(jnp.float32)
        scaled = (hidden_f * gain_own[None, :]).astype(jnp.bfloat16)
        squares = exchange_sum(jnp.sum(hidden_f * hidden_f, axis=1), "tp", count)
        chunk = rows // (PERIODS * STREAMS)

        labels = jnp.arange(DOCS, dtype=jnp.int32)
        starts = exchange_sum(
            jnp.sum((doc_ids[None, :] < labels[:, None]).astype(jnp.int32), axis=1), "sp", sp_count
        )
        pack = rows * 2 * HD // width
        packed = count == 4 and chunk == 2 * pack
        kv_info = jnp.stack([rank, rank, rank, jnp.int32(heads)]).astype(jnp.int32)
        if packed:
            ends, across, swap, kv_own = kv_terms_of(
                (
                    lambda r: (3 - r, jnp.where(r == 0, 2, 1)),
                    lambda r: (jnp.where(r == 1, 3, 0), jnp.where(r == 1, 2, 1)),
                    lambda r: (r ^ 1,),
                    lambda r: (r,),
                ),
                kv_info,
                after(scaled, squares),
                w_key,
                w_value,
            )
        else:
            (kv_terms,) = kv_terms_of((lambda r: tuple(range(count)),), kv_info, scaled, w_key, w_value)
            kv_terms = kv_terms.reshape(count, pack, width)

        def positions():
            base = sp_rank * rows
            own_index = base + jnp.arange(rows, dtype=jnp.int32)
            first = jnp.sum(
                jnp.where(doc_ids[:, None] == labels[None, :], starts[None, :], 0), axis=1
            )
            cosine, sine = rope_tables(own_index - first)
            inverse = lax.rsqrt(squares / model + norm_eps)[:, None]
            table = jnp.concatenate(
                [
                    cosine * inverse,
                    sine * inverse,
                    jnp.broadcast_to(first.astype(jnp.float32)[:, None], (rows, HD)),
                    jnp.broadcast_to(inverse, (rows, HD)),
                ],
                axis=1,
            )
            infos = [
                jnp.stack([rank, first[k * STREAMS * chunk] // BLOCK, sp_rank]).astype(jnp.int32)
                for k in range(PERIODS)
            ]
            return table, infos

        out = None
        kv_pieces = None
        last = [(None, None)] * STREAMS
        terms = [None] * STREAMS
        firsts = [None] * STREAMS
        history = []
        for period in range(PERIODS + 1):
            gather = period < PERIODS
            owns = [None] * STREAMS
            arrived = [[] for _ in range(STREAMS)]
            for step in range(1, count + 1):
                for j in range(STREAMS):
                    if not (gather and step < count) and not (firsts[j] is not None and step > 1):
                        continue
                    if gather and step == 1:
                        low = (period * STREAMS + j) * chunk
                        owns[j] = scaled[low : low + chunk]
                    earlier = [history[-STREAMS - 1 : -STREAMS], last[j]]

                    last[j] = line.round(step, owns[j], terms[j], firsts[j], last[j], earlier)
                    history.append(last[j])
                    if firsts[j] is not None and j == 0 and step == 2:
                        terms = output_terms(count, STREAMS, after(flat, last[j]), w_out)
                    if gather and step < count:
                        arrived[j].append(("outer", step, last[j][0]))
                        if step < count - 1:
                            arrived[j].append(("inner", step, last[j][1]))
                    if packed and period == 0 and j == STREAMS - 1 and step == 1:
                        met = line.outer(ends, 1, gather=False)
                        crossed = line.inner(after(line.add(across, met), last[j]))
                    if packed and period == 0 and j == STREAMS - 1 and step == 2:
                        mine = jnp.where(line.middle, line.add(swap, crossed[:pack]), swap)
                        met = line.outer(after(mine, last[j])).astype(jnp.float32)
                        kv = kv_own.astype(jnp.float32) + met
                        kv = jnp.where(line.middle, kv + crossed[pack:].astype(jnp.float32), kv)
            if period == 0:
                table, infos = positions()
                if not packed:
                    kv = line.scatter(kv_terms, history[-1])
                kv = kv_total(kv, table)
                kv_pieces = [kv] + [
                    lax.ppermute(kv, "sp", [(i, i ^ d) for i in range(sp_count)])
                    for d in range(1, sp_count)
                ]
            for j in range(STREAMS):
                if period > 0:
                    low = ((period - 1) * STREAMS + j) * chunk
                    out = finish(count, low, infos[0], hidden, terms[j], last[j], out)
            if gather:
                low = period * STREAMS * chunk
                *firsts, flat = chunk_terms(
                    count, low, chunk, scaled, arrived, infos[period], w_query, w_out, table, kv_pieces
                )
                terms = [None] * STREAMS
        return out

    return body


def solution(mesh):
    placed = (
        P(("rep", "sp"), "tp"),
        P(("rep", "sp")),
        P(),
        P(None, "tp"),
        P("tp", None),
        P("tp", None),
        P("tp", None),
    )
    body = make_body(mesh.shape["tp"], mesh.shape["sp"])
    return jax.shard_map(
        body, mesh=mesh, in_specs=placed, out_specs=P(("rep", "sp"), "tp"), check_vma=False
    )
```

```python
import functools

import jax
import jax.numpy as jnp
from jax import lax
from jax.experimental import pallas as pl
from jax.experimental.pallas import tpu as pltpu
from jax.sharding import PartitionSpec as P

HD = 128
HQ = 32
KV = 4
DOCS = 4
PERIODS = 2
STREAMS = 2

rope_base = 500000.0
norm_eps = 1e-05
masked_score = -1e30
log2_e = 1.4426950408889634
VMEM_LIMIT = 42 * 1024 * 1024
GROUP = 2
BLOCK = 512
VMEM = pl.BlockSpec(memory_space=pltpu.VMEM)
SMEM = pl.BlockSpec(memory_space=pltpu.SMEM)
ANY = pl.BlockSpec(memory_space=pl.ANY)


def rope_tables(positions):
    half_dim = HD // 2
    steps_index = jnp.arange(half_dim, dtype=jnp.float32)
    frequency = jnp.power(rope_base, -2.0 * steps_index / HD)
    angles = positions.astype(jnp.float32)[:, None] * frequency[None, :]
    cosine, sine = jnp.cos(angles), jnp.sin(angles)
    return jnp.concatenate([cosine, cosine], axis=1), jnp.concatenate([-sine, sine], axis=1)


def rotate(field, cosine, sine):
    half_dim = HD // 2
    swapped = jnp.concatenate([field[..., half_dim:], field[..., :half_dim]], axis=-1)
    return field * cosine + swapped * sine


def in_hbm(value):
    return pltpu.with_memory_space_constraint(value, pltpu.HBM)


def wait_for(target, sem):
    pltpu.make_async_copy(target, target, sem).wait()


def chunk_kernel(count, pieces_of, low, info_ref, scaled, *refs):
    streams = len(pieces_of)
    kept = []
    for of in pieces_of:
        kept.append(refs[: len(of)])
        refs = refs[len(of) :]
    w_query, w_out, table = refs[:3]
    outs, refs = refs[-12 - streams : -12], refs[3 : -12 - streams] + refs[-12:]
    kv_pieces = refs[:-12]
    flat, held, query_w, out_w, rows_table, kv, query, top, acc, sems, q_sems, o_sems = refs[-12:]
    rows = held.shape[0]
    each = rows // streams
    width = held.shape[1] // count
    parts, depth, piece_columns = query_w.shape[0], query_w.shape[1], query_w.shape[2]
    heads = query.shape[0] // rows
    rank, start, sp_rank = info_ref[0], info_ref[1], info_ref[2]
    span = kv_pieces[0].shape[0]
    base = sp_rank * span
    even = rank % 2 == 0

    def place(source, first_row, count_rows, block):
        columns = pl.ds(pl.multiple_of(block * width, width), width)
        target = held.at[first_row : first_row + count_rows, columns]
        return pltpu.make_async_copy(source, target, sems.at[0])

    place(scaled.at[pl.ds(low, rows)], 0, rows, rank).start()
    for j in range(streams):
        for piece, (kind, step) in zip(kept[j], pieces_of[j]):
            block = jnp.where(even == (kind == "outer"), rank + step, rank - step)

            @pl.when((block >= 0) & (block < count))
            def _():
                place(piece, j * each, each, block).start()

    def query_copy(k):
        return pltpu.make_async_copy(
            w_query.at[:, pl.ds(pl.multiple_of(k * piece_columns, piece_columns), piece_columns)],
            query_w.at[k],
            q_sems.at[k * q_sems.shape[0] // parts],
        )

    for k in range(parts):
        query_copy(k).start()
    table_copy = pltpu.make_async_copy(table.at[pl.ds(low, rows)], rows_table, sems.at[1])
    table_copy.start()
    kv_copies = [
        pltpu.make_async_copy(
            piece,
            kv.at[pl.ds(pl.multiple_of((sp_rank ^ d) * span, span), span)],
            sems.at[2],
        )
        for d, piece in enumerate(kv_pieces)
    ]
    for copy in kv_copies:
        copy.start()
    out_parts = out_w.shape[0]
    out_columns = out_w.shape[2]
    far = jnp.where(rank < count // 2, count - 1, 0)

    def out_copy(k):
        at = pl.multiple_of(far * width + k * out_columns, out_columns)
        return pltpu.make_async_copy(w_out.at[:, pl.ds(at, out_columns)], out_w.at[k], o_sems.at[k])

    wait_for(held, sems.at[0])
    table_copy.wait()
    factor = HD ** (-0.5) * log2_e
    cos, sin = rows_table[:, :HD] * factor, rows_table[:, HD : 2 * HD] * factor
    pair = piece_columns // HD

    @pl.loop(0, parts)
    def _(k):
        query_copy(k).wait()

        @pl.when(k == 0)
        def _():
            for i in range(out_parts):
                out_copy(i).start()

        total = jnp.dot(held[...], query_w[k], preferred_element_type=jnp.float32)
        for h in range(pair):
            field = total[:, h * HD : (h + 1) * HD]
            swapped = pltpu.roll(field, HD // 2, 1)
            at = pl.multiple_of((k * pair + h) * rows, rows)
            query[pl.ds(at, rows), :] = (field * cos + swapped * sin).astype(jnp.bfloat16)

    wait_for(kv, sems.at[2])
    top[...] = jnp.full_like(top, masked_score)
    acc[...] = jnp.zeros_like(acc)
    first = rows_table[:, 2 * HD : 2 * HD + 1].astype(jnp.int32)
    row_index = base + low + lax.broadcasted_iota(jnp.int32, (rows, BLOCK), 0)
    column = lax.broadcasted_iota(jnp.int32, (rows, BLOCK), 1)
    ones = jnp.ones((BLOCK, HD), jnp.bfloat16)
    together = min(heads, GROUP)

    tail = (low + rows - 1) % BLOCK + 1 if span % BLOCK == 0 else BLOCK

    def step(j, carry, size=BLOCK):
        offset = pl.multiple_of(j * BLOCK, BLOCK)
        key_index = column[:, :size] + offset
        bias = jnp.where(
            (key_index <= row_index[:, :size]) & (key_index >= first), 0.0, masked_score
        )
        key = kv[pl.ds(offset, size), :HD]
        value = jnp.concatenate([kv[pl.ds(offset, size), HD:], ones[:size]], axis=1)
        for g in range(heads // together):
            at = slice(g * together * rows, (g + 1) * together * rows)
            scores = lax.dot_general(
                query[at], key, (((1,), (1,)), ((), ())), preferred_element_type=jnp.float32
            )
            scores = (scores.reshape(together, rows, size) + bias[None]).reshape(-1, size)
            old = top[at]
            new = jnp.maximum(old, jnp.max(scores, axis=1, keepdims=True))
            exps = jnp.exp2(scores - new[:, :1]).astype(jnp.bfloat16)
            mixed = jnp.dot(exps, value, preferred_element_type=jnp.float32)
            keep = jnp.exp2(old - new)
            acc[at] = acc[at] * jnp.concatenate([keep, keep], axis=1) + mixed
            top[at] = new
        return carry

    final = (base + low + rows - 1) // BLOCK
    lax.fori_loop(start, final, step, 0)
    step(final, 0, tail)
    for h in range(heads):
        span = slice(h * rows, (h + 1) * rows)
        flat[:, h * HD : (h + 1) * HD] = (acc[span, :HD] / acc[span, HD:]).astype(jnp.bfloat16)

    for k in range(out_parts):
        out_copy(k).wait()
        mixed = jnp.dot(flat[...], out_w[k], preferred_element_type=jnp.float32)
        for j in range(streams):
            outs[j][:, k * out_columns : (k + 1) * out_columns] = mixed[
                j * each : (j + 1) * each
            ].astype(jnp.bfloat16)


def output_kernel(flat, w_out, *refs):
    outs, weight, sems = refs[:-2], refs[-2], refs[-1]
    count, each, width = outs[0].shape
    parts, _, columns = weight.shape
    per_block = parts // count

    def copy(k):
        at = pl.multiple_of(k * columns, columns)
        return pltpu.make_async_copy(w_out.at[:, pl.ds(at, columns)], weight.at[k], sems.at[k])

    for k in range(parts):
        copy(k).start()

    @pl.loop(0, count)
    def _(b):
        for k in range(per_block):
            copy(b * per_block + k).wait()
            mixed = jnp.dot(flat[...], weight[b * per_block + k], preferred_element_type=jnp.float32)
            for j, out in enumerate(outs):
                out[b, :, k * columns : (k + 1) * columns] = mixed[j * each : (j + 1) * each].astype(
                    jnp.bfloat16
                )


def output_terms(count, streams, flat, w_out):
    rows, inner = flat.shape
    width = w_out.shape[1] // count
    columns = min(width, 1024)
    parts = w_out.shape[1] // columns
    return pl.pallas_call(
        output_kernel,
        out_shape=[jax.ShapeDtypeStruct((count, rows // streams, width), jnp.bfloat16)] * streams,
        in_specs=[VMEM, ANY],
        out_specs=[VMEM] * streams,
        scratch_shapes=[
            pltpu.VMEM((parts, inner, columns), jnp.bfloat16),
            pltpu.SemaphoreType.DMA((parts,)),
        ],
        compiler_params=pltpu.CompilerParams(vmem_limit_bytes=VMEM_LIMIT),
        cost_estimate=pl.CostEstimate(
            flops=rows * inner * width * count, bytes_accessed=0, transcendentals=0
        ),
        name="output_terms",
    )(flat, in_hbm(w_out))


def chunk_terms(count, low, each, scaled, arrived, info, w_query, w_out, table, kv_pieces):
    rows = each * len(arrived)
    width = scaled.shape[1]
    model, columns = w_query.shape
    inner = w_out.shape[0]
    heads = columns // HD
    tokens = kv_pieces[0].shape[0] * len(kv_pieces)
    pieces = [scaled] + [piece for of in arrived for _, _, piece in of]
    pieces_of = [[(kind, step) for kind, step, _ in of] for of in arrived]
    q_columns = min(columns, 256)
    o_columns = min(width, 1024)
    q_parts, o_parts = columns // q_columns, width // o_columns
    return pl.pallas_call(
        functools.partial(chunk_kernel, count, pieces_of, low),
        out_shape=[jax.ShapeDtypeStruct((each, width), jnp.bfloat16)] * len(arrived)
        + [jax.ShapeDtypeStruct((rows, inner), jnp.bfloat16)],
        in_specs=[SMEM] + [ANY] * (len(pieces) + 3 + len(kv_pieces)),
        out_specs=[VMEM] * (len(arrived) + 1),
        scratch_shapes=[
            pltpu.VMEM((rows, model), jnp.bfloat16),
            pltpu.VMEM((q_parts, model, q_columns), jnp.bfloat16),
            pltpu.VMEM((o_parts, inner, o_columns), jnp.bfloat16),
            pltpu.VMEM((rows, table.shape[1]), jnp.float32),
            pltpu.VMEM((tokens, 2 * HD), jnp.bfloat16),
            pltpu.VMEM((heads * rows, HD), jnp.bfloat16),
            pltpu.VMEM((heads * rows, HD), jnp.float32),
            pltpu.VMEM((heads * rows, 2 * HD), jnp.float32),
            pltpu.SemaphoreType.DMA((3,)),
            pltpu.SemaphoreType.DMA((q_parts,)),
            pltpu.SemaphoreType.DMA((o_parts,)),
        ],
        compiler_params=pltpu.CompilerParams(vmem_limit_bytes=VMEM_LIMIT),
        cost_estimate=pl.CostEstimate(flops=rows * model * columns, bytes_accessed=0, transcendentals=0),
        name="chunk_terms",
    )(info, *[in_hbm(x) for x in (*pieces, w_query, w_out, table, *kv_pieces)])


def kv_kernel(group, slots, info_ref, scaled, w_key, w_value, *refs):
    outs = refs[: len(slots)]
    held, key_w, value_w, key, value, sems = refs[len(slots) :]
    copies = [
        pltpu.make_async_copy(source, target, sems.at[k])
        for k, (source, target) in enumerate(((scaled, held), (w_key, key_w), (w_value, value_w)))
    ]
    for copy in copies:
        copy.start()
    copies[0].wait()
    copies[1].wait()
    key[...] = jnp.dot(held[...], key_w[...], preferred_element_type=jnp.float32).astype(jnp.bfloat16)
    copies[2].wait()
    value[...] = jnp.dot(held[...], value_w[...], preferred_element_type=jnp.float32).astype(jnp.bfloat16)
    width = outs[0].shape[-1]
    rows = key.shape[0] * 2 * HD // width
    for out, devices in zip(outs, slots):
        for n, device in enumerate(devices(info_ref[0])):
            columns = pl.ds(pl.multiple_of(device * info_ref[3] // group * HD, HD), HD)
            for i in range(width // (2 * HD)):
                at = i * 2 * HD
                span = slice(i * rows, (i + 1) * rows)
                out[n * rows : (n + 1) * rows, at : at + HD] = key[span, columns]
                out[n * rows : (n + 1) * rows, at + HD : at + 2 * HD] = value[span, columns]


def kv_terms_of(slots, info, scaled, w_key, w_value):
    rows, width = scaled.shape
    columns = w_key.shape[1]
    pack = rows * 2 * HD // width
    shapes = [
        jax.ShapeDtypeStruct((pack * len(devices(0)), width), jnp.bfloat16) for devices in slots
    ]
    return pl.pallas_call(
        functools.partial(kv_kernel, HQ // KV, slots),
        out_shape=shapes,
        in_specs=[SMEM] + [ANY] * 3,
        out_specs=[VMEM] * len(slots),
        scratch_shapes=[
            pltpu.VMEM((rows, width), jnp.bfloat16),
            pltpu.VMEM((width, columns), jnp.bfloat16),
            pltpu.VMEM((width, columns), jnp.bfloat16),
            pltpu.VMEM((rows, columns), jnp.bfloat16),
            pltpu.VMEM((rows, columns), jnp.bfloat16),
            pltpu.SemaphoreType.DMA((3,)),
        ],
        compiler_params=pltpu.CompilerParams(vmem_limit_bytes=VMEM_LIMIT),
        cost_estimate=pl.CostEstimate(flops=0, bytes_accessed=2 * rows * width, transcendentals=0),
        name="kv_terms",
    )(info, in_hbm(scaled), in_hbm(w_key), in_hbm(w_value))


def kv_total_kernel(packed, table, out):
    rows, width = packed.shape
    for i in range(width // (2 * HD)):
        at = i * 2 * HD
        span = slice(i * rows, (i + 1) * rows)
        key, value = packed[:, at : at + HD], packed[:, at + HD : at + 2 * HD]
        rotated = key * table[span, :HD] + pltpu.roll(key, HD // 2, 1) * table[span, HD : 2 * HD]
        out[span, :HD] = rotated.astype(jnp.bfloat16)
        out[span, HD:] = (value * table[span, 3 * HD :]).astype(jnp.bfloat16)


def kv_total(packed, table):
    return pl.pallas_call(
        kv_total_kernel,
        out_shape=jax.ShapeDtypeStruct((table.shape[0], 2 * HD), jnp.bfloat16),
        in_specs=[VMEM] * 2,
        out_specs=VMEM,
        compiler_params=pltpu.CompilerParams(vmem_limit_bytes=VMEM_LIMIT),
        cost_estimate=pl.CostEstimate(flops=0, bytes_accessed=8 * packed.size, transcendentals=0),
        name="kv_total",
    )(packed, table)


def finish_kernel(count, low, has_inner, info_ref, hidden, terms, outer, inner, *refs):
    out, a, b, c, d, total, sems = refs[-7:]
    rows = a.shape[0]
    rank = info_ref[0]
    copies = [
        pltpu.make_async_copy(source, target, sems.at[k])
        for k, (source, target) in enumerate(
            [(hidden.at[pl.ds(low, rows)], a), (terms.at[rank], b), (outer, c), (inner, d)]
        )
    ]
    for copy in copies:
        copy.start()
    for copy in copies:
        copy.wait()
    summed = b[...].astype(jnp.float32) + c[...].astype(jnp.float32)
    middle = (rank > 0) & (rank < count - 1)
    other = jnp.where(middle, d[...].astype(jnp.float32), 0.0)
    total[...] = (a[...].astype(jnp.float32) + (summed + other)).astype(jnp.bfloat16)
    copy = pltpu.make_async_copy(total, out.at[pl.ds(low, rows)], sems.at[4])
    copy.start()
    copy.wait()


def finish(count, low, info, hidden, terms, last, out):
    _, rows, width = terms.shape
    outer, inner = last
    operands = [info, hidden, terms, outer, inner if inner is not None else outer]
    aliases = {}
    if out is not None:
        aliases = {len(operands): 0}
        operands.append(out)
    return pl.pallas_call(
        functools.partial(finish_kernel, count, low, inner is not None),
        out_shape=jax.ShapeDtypeStruct(hidden.shape, jnp.bfloat16),
        in_specs=[SMEM] + [ANY] * (len(operands) - 1),
        out_specs=ANY,
        scratch_shapes=[pltpu.VMEM((rows, width), jnp.bfloat16)] * 5 + [pltpu.SemaphoreType.DMA((5,))],
        input_output_aliases=aliases,
        cost_estimate=pl.CostEstimate(flops=0, bytes_accessed=6 * rows * width, transcendentals=0),
        compiler_params=pltpu.CompilerParams(vmem_limit_bytes=VMEM_LIMIT),
        name="finish",
    )(*operands)


def after(value, others):
    return lax.optimization_barrier((value, others))[0]


def exchange_sum(value, axis, size):
    parts = [lax.ppermute(value, axis, [(i, i ^ d) for i in range(size)]) for d in range(1, size)]
    return sum(parts, value)


class Line:
    def __init__(self, count, sp_count, rank):
        self.count, self.rank = count, rank
        self.even = rank % 2 == 0
        self.middle = (rank > 0) & (rank < count - 1)
        self.outer_pairs = [(i, i ^ 1) for i in range(count)]
        self.inner_pairs = []
        for i in range(count):
            for s in range(sp_count):
                partner = i + 1 if i % 2 else i - 1
                if 0 < i < count - 1:
                    self.inner_pairs.append((i * sp_count + s, partner * sp_count + s))
                else:
                    self.inner_pairs.append((i * sp_count + s, i * sp_count + (s ^ 1)))

    def outer(self, value, step=None, gather=True):
        pairs = self.outer_pairs
        if step is not None and gather:
            pairs = [
                (i, p) for i, p in pairs if (i >= step - 1 if i % 2 == 0 else i <= self.count - step)
            ]
        elif step is not None:
            pairs = [
                (i, p) for i, p in pairs if (i <= step - 1 if i % 2 == 0 else i >= self.count - step)
            ]
        return lax.ppermute(value, "tp", pairs)

    def inner(self, value):
        return lax.ppermute(value, ("tp", "sp"), self.inner_pairs)

    def term(self, terms, upward, step):
        dest = jnp.where(upward, self.rank + self.count - step, self.rank - self.count + step)
        valid = (dest >= 0) & (dest < self.count)
        if terms is None:
            return None, valid
        return lax.dynamic_index_in_dim(terms, jnp.clip(dest, 0, self.count - 1), 0, False), valid

    def round(self, step, own, terms, first, last, earlier):
        count = self.count
        from_outer, from_inner = last
        gather_outer = own is not None and step < count
        gather_inner = own is not None and step < count - 1
        scatter_outer = first is not None and step > 1
        scatter_inner = first is not None and step > 2
        to_outer = to_inner = None
        if gather_outer:
            to_outer = own if step == 1 else from_inner
        if gather_inner:
            to_inner = own if step == 1 else from_outer
        if scatter_outer:
            mine, valid = self.term(terms, self.even, step - 1)
            if step == 2:
                mine = first
            if step > 3:
                added = (mine.astype(jnp.float32) + from_inner.astype(jnp.float32)).astype(jnp.bfloat16)
                mine = jnp.where(self.middle, added, mine)
            to_outer = mine if to_outer is None else jnp.where(valid, mine, to_outer)
        if scatter_inner:
            mine, valid = self.term(terms, ~self.even, step - 1)
            mine = (mine.astype(jnp.float32) + from_outer.astype(jnp.float32)).astype(jnp.bfloat16)
            to_inner = mine if to_inner is None else jnp.where(valid, mine, to_inner)
        to_outer, to_inner = after((to_outer, to_inner), earlier)
        alone = step if first is None and step > 1 else None
        got_outer = None if to_outer is None else self.outer(to_outer, alone)
        got_inner = None if to_inner is None else self.inner(to_inner)
        return got_outer, got_inner

    def scatter(self, terms, earlier):
        last = (None, None)
        for step in range(2, self.count + 1):
            last = self.round(step, None, terms, self.term(terms, self.even, 1)[0], last, earlier)
        return self.total(terms, last)

    def add(self, a, b):
        return (a.astype(jnp.float32) + b.astype(jnp.float32)).astype(jnp.bfloat16)

    def total(self, terms, last):
        mine = lax.dynamic_index_in_dim(terms, self.rank, 0, False).astype(jnp.float32)
        mine = mine + last[0].astype(jnp.float32)
        return jnp.where(self.middle, mine + last[1].astype(jnp.float32), mine)


def make_body(count, sp_count):
    def body(hidden, doc_ids, gain, w_query, w_key, w_value, w_out):
        rows, width = hidden.shape
        rank = lax.axis_index("tp")
        sp_rank = lax.axis_index("sp")
        heads = w_query.shape[1] // HD
        group = HQ // KV
        model = width * count
        line = Line(count, sp_count, rank)
        gain_own = lax.dynamic_slice_in_dim(gain, rank * width, width, 0).astype(jnp.float32)
        hidden_f = hidden.astype(jnp.float32)
        scaled = (hidden_f * gain_own[None, :]).astype(jnp.bfloat16)
        squares = exchange_sum(jnp.sum(hidden_f * hidden_f, axis=1), "tp", count)
        chunk = rows // (PERIODS * STREAMS)

        labels = jnp.arange(DOCS, dtype=jnp.int32)
        starts = exchange_sum(
            jnp.sum((doc_ids[None, :] < labels[:, None]).astype(jnp.int32), axis=1), "sp", sp_count
        )
        pack = rows * 2 * HD // width
        packed = count == 4 and chunk == 2 * pack
        kv_info = jnp.stack([rank, rank, rank, jnp.int32(heads)]).astype(jnp.int32)
        if packed:
            ends, across, swap, kv_own = kv_terms_of(
                (
                    lambda r: (3 - r, jnp.where(r == 0, 2, 1)),
                    lambda r: (jnp.where(r == 1, 3, 0), jnp.where(r == 1, 2, 1)),
                    lambda r: (r ^ 1,),
                    lambda r: (r,),
                ),
                kv_info,
                after(scaled, squares),
                w_key,
                w_value,
            )
        else:
            (kv_terms,) = kv_terms_of((lambda r: tuple(range(count)),), kv_info, scaled, w_key, w_value)
            kv_terms = kv_terms.reshape(count, pack, width)

        def positions():
            base = sp_rank * rows
            own_index = base + jnp.arange(rows, dtype=jnp.int32)
            first = jnp.sum(
                jnp.where(doc_ids[:, None] == labels[None, :], starts[None, :], 0), axis=1
            )
            cosine, sine = rope_tables(own_index - first)
            inverse = lax.rsqrt(squares / model + norm_eps)[:, None]
            table = jnp.concatenate(
                [
                    cosine * inverse,
                    sine * inverse,
                    jnp.broadcast_to(first.astype(jnp.float32)[:, None], (rows, HD)),
                    jnp.broadcast_to(inverse, (rows, HD)),
                ],
                axis=1,
            )
            infos = [
                jnp.stack([rank, first[k * STREAMS * chunk] // BLOCK, sp_rank]).astype(jnp.int32)
                for k in range(PERIODS)
            ]
            return table, infos

        out = None
        kv_pieces = None
        last = [(None, None)] * STREAMS
        terms = [None] * STREAMS
        firsts = [None] * STREAMS
        history = []
        for period in range(PERIODS + 1):
            gather = period < PERIODS
            owns = [None] * STREAMS
            arrived = [[] for _ in range(STREAMS)]
            for step in range(1, count + 1):
                for j in range(STREAMS):
                    if not (gather and step < count) and not (firsts[j] is not None and step > 1):
                        continue
                    if gather and step == 1:
                        low = (period * STREAMS + j) * chunk
                        owns[j] = scaled[low : low + chunk]
                    earlier = [history[-STREAMS - 1 : -STREAMS], last[j]]

                    last[j] = line.round(step, owns[j], terms[j], firsts[j], last[j], earlier)
                    history.append(last[j])
                    if firsts[j] is not None and j == 0 and step == 2:
                        terms = output_terms(count, STREAMS, after(flat, last[j]), w_out)
                    if gather and step < count:
                        arrived[j].append(("outer", step, last[j][0]))
                        if step < count - 1:
                            arrived[j].append(("inner", step, last[j][1]))
                    if packed and period == 0 and j == STREAMS - 1 and step == 1:
                        met = line.outer(ends, 1, gather=False)
                        crossed = line.inner(after(line.add(across, met), last[j]))
                    if packed and period == 0 and j == STREAMS - 1 and step == 2:
                        mine = jnp.where(line.middle, line.add(swap, crossed[:pack]), swap)
                        met = line.outer(after(mine, last[j])).astype(jnp.float32)
                        kv = kv_own.astype(jnp.float32) + met
                        kv = jnp.where(line.middle, kv + crossed[pack:].astype(jnp.float32), kv)
            if period == 0:
                table, infos = positions()
                if not packed:
                    kv = line.scatter(kv_terms, history[-1])
                kv = kv_total(kv, table)
                kv_pieces = [kv] + [
                    lax.ppermute(kv, "sp", [(i, i ^ d) for i in range(sp_count)])
                    for d in range(1, sp_count)
                ]
            for j in range(STREAMS):
                if period > 0:
                    low = ((period - 1) * STREAMS + j) * chunk
                    out = finish(count, low, infos[0], hidden, terms[j], last[j], out)
            if gather:
                low = period * STREAMS * chunk
                *firsts, flat = chunk_terms(
                    count, low, chunk, scaled, arrived, infos[period], w_query, w_out, table, kv_pieces
                )
                terms = [None] * STREAMS
        return out

    return body


def solution(mesh):
    placed = (
        P(("rep", "sp"), "tp"),
        P(("rep", "sp")),
        P(),
        P(None, "tp"),
        P("tp", None),
        P("tp", None),
        P("tp", None),
    )
    body = make_body(mesh.shape["tp"], mesh.shape["sp"])
    return jax.shard_map(
        body, mesh=mesh, in_specs=placed, out_specs=P(("rep", "sp"), "tp"), check_vma=False
    )
```
